512 devices in a mesh: lat: 32 (over x, y, core), lon: 16 (over z).
Axes of the slice: x: 4, y: 4, z: 16, core: 2. Of those that a mesh axis runs over, the one named last changes fastest.
Arguments:
- grid_in: bfloat16 [384, 768, 384], P('lat', 'lon'), may hold values from -6 to 6
- grid_cot: bfloat16 [384, 768, 384], P('lat', 'lon'), may hold values from -6 to 6
- legendre: bfloat16 [384, 384, 384], P('lat'), as said below
- filters: float32 [384, 2, 384], P(None, None, 'lon'), may hold values from -6 to 6
Outputs:
- grad_grid: bfloat16 [384, 768, 384], P('lat', 'lon')
- grad_filters: float32 [384, 2, 384], P('lat', None, 'lon')
The draws below stay inside these ranges and needn't reach their ends.
Inputs may be any that keep to these rules, and one draw needn't show every extreme that they name: legendre[m, q, l] is zero wherever the degree l is below the order m.
All inputs are finite; a program needn't handle non-finite values.
Results may differ from the reference program's by a relative error of at most 0.008.
Values may be sent and summed in bfloat16 or wider, within the bound.
A program may use at most 64 MiB of HBM per device.

```python
import math
import jax
import jax.numpy as jnp
from jax import lax

LATS = 384
LONS = 768
DEGREES = 384
CHANNELS = 384


def draw_legendre(key, part):
    key = jax.random.fold_in(key, 7)
    values = jax.random.normal(key, (DEGREES, LATS, DEGREES), jnp.float32)
    order_at = lax.broadcasted_iota(jnp.int32, (DEGREES, LATS, DEGREES), 0)
    degree_at = lax.broadcasted_iota(jnp.int32, (DEGREES, LATS, DEGREES), 2)
    scaled = values * LATS ** (-0.5)
    return jnp.where(degree_at >= order_at, scaled, jnp.zeros_like(scaled)).astype(jnp.bfloat16)


def shard_levels(rng, dims, pieces, low, top_value):
    gain, own = 1.0, jax.random.fold_in(rng, 6)
    for dim, shards_of in pieces:
        draws = jnp.exp(jax.random.uniform(jax.random.fold_in(own, dim), (shards_of,), jnp.float32, low / len(pieces), top_value / len(pieces)))
        gain = gain * jnp.repeat(draws, dims[dim] // shards_of).reshape([-1 if axis == dim else 1 for axis in range(len(dims))])
    return gain


def scatter_about(key, extent, width, most, shards=(), kind=jnp.bfloat16):
    entries = jax.random.normal(key, extent, jnp.float32) * width
    if len(shards) > 0:
        entries = shard_levels(key, extent, shards, -0.22, 0.18) * entries
    return jnp.clip(entries, min=-most, max=most).astype(kind)


def setup_inputs(seed: int = 0) -> dict:
    arg_keys = jax.random.split(jax.random.key(seed), 5)
    grid_in = scatter_about(arg_keys[0], (LATS, LONS, CHANNELS), 1.0, 6.0, ((0, 32), (1, 16)))
    grid_cot = scatter_about(arg_keys[1], (LATS, LONS, CHANNELS), 1.0, 6.0, ((0, 32), (1, 16)))
    legendre = draw_legendre(jax.random.fold_in(arg_keys[4], 71), 0)
    filters = scatter_about(arg_keys[3], (DEGREES, 2, CHANNELS), 1.0, 6.0, ((2, 16),), jnp.float32)
    return dict(grid_in=grid_in, grid_cot=grid_cot, legendre=legendre, filters=filters)


def fourier_table(points, degrees):
    points_at = lax.broadcasted_iota(jnp.int32, (points, degrees), 0)
    wave_num = lax.broadcasted_iota(jnp.int32, (points, degrees), 1)
    phases = (points_at * wave_num) % points
    angles = phases.astype(jnp.float32) * (2.0 * math.pi / points)
    fourier = jnp.stack([jnp.cos(angles), -jnp.sin(angles)], axis=2) * (points ** -0.5)
    return fourier.reshape(points, 2 * degrees).astype(jnp.bfloat16)


def reference(grid_in, grid_cot, legendre, filters):
    four_wide = fourier_table(LONS, DEGREES).astype(jnp.float32)
    table_wide = legendre.astype(jnp.float32)

    def analysis(grid):
        spectra = jnp.einsum("qnc,nk->qck", grid.astype(jnp.float32), four_wide).astype(jnp.bfloat16)
        shaped = spectra.astype(jnp.float32).reshape(LATS, CHANNELS, DEGREES, 2)
        return jnp.einsum("oql,qcor->olrc", table_wide, shaped)

    coeff_in = analysis(grid_in)
    coeff_cot = analysis(grid_cot)
    in_re, in_im = coeff_in[:, :, 0, :], coeff_in[:, :, 1, :]
    cot_re, cot_im = coeff_cot[:, :, 0, :], coeff_cot[:, :, 1, :]
    grad_filters = jnp.stack([jnp.sum(in_re * cot_re + in_im * cot_im, axis=0),
                              jnp.sum(in_re * cot_im - in_im * cot_re, axis=0)], axis=1)
    gain_re, gain_im = filters[:, 0, :], filters[:, 1, :]
    back = jnp.stack([gain_re * cot_re + gain_im * cot_im,
                      gain_re * cot_im - gain_im * cot_re], axis=2).astype(jnp.bfloat16)
    spec_back = jnp.einsum("oql,olrc->qcor", table_wide, back.astype(jnp.float32))
    spec_back = spec_back.astype(jnp.bfloat16).reshape(LATS, CHANNELS, 2 * DEGREES)
    grad_grid = jnp.einsum("qck,nk->qnc", spec_back.astype(jnp.float32), four_wide).astype(jnp.bfloat16)
    return grad_grid, grad_filters
```

```python
import math

import jax
import jax.numpy as jnp
import ml_dtypes
import numpy as np
from jax import lax
from jax.experimental import pallas as pl
from jax.experimental.pallas import tpu as pltpu
from jax.sharding import PartitionSpec as P

MESH = pl.DeviceIdType.MESH
BF16 = jnp.bfloat16
F32 = jnp.float32

NZ, NL = 16, 32
LATS, LONS, DEGREES, CHANNELS = 384, 768, 384, 384
Q, N, C = LATS // NL, LONS // NZ, CHANNELS // NZ
M = DEGREES // NL
RING = 384
GROUPS = N // 16

PARTS = ((0, 7), (7, 5))
WIDTH = tuple(C * rows for _, rows in PARTS)
TILES = tuple(-(-GROUPS * w // 128) for w in WIDTH)


def fourier_tables():
    points = np.arange(LONS, dtype=np.int64)[:, None]
    order = np.arange(DEGREES, dtype=np.int64)[None, :]
    phases = (points * order) % LONS
    angles = phases.astype(np.float32) * np.float32(2.0 * math.pi / LONS)
    pair = np.stack([np.cos(angles), -np.sin(angles)], axis=2) * np.float32(LONS ** (-0.5))
    table = pair.reshape(LONS, 2 * DEGREES).astype(ml_dtypes.bfloat16)
    n_of = np.arange(LONS).reshape(NZ, GROUPS, 16).transpose(1, 0, 2).reshape(-1)
    k = np.arange(2 * DEGREES).reshape(NL, 2 * M)
    k_of = np.concatenate([k[:, :16].reshape(-1), k[:, 16:].reshape(-1)])
    back = table[n_of][:, k_of]
    return np.ascontiguousarray(back.T), np.ascontiguousarray(back)


def lanes(rows):
    return lax.broadcasted_iota(jnp.int32, (rows, 128), 1)


def merge_blocks(rows, pick):
    at = lanes(rows)
    tiles = []
    for t in range(3):
        value = None
        for b in range(16):
            low, high = C * b - 128 * t, C * (b + 1) - 128 * t
            if high <= 0 or low >= 128:
                continue
            block = pick(b, t)
            value = block if value is None else jnp.where(at >= low, block, value)
        tiles.append(value)
    return jnp.concatenate(tiles, axis=1)


def block_transpose(rows, count, load, store):
    zero = jnp.zeros((rows, 128), F32)
    for x in range(count):
        ring = merge_blocks(
            rows, lambda b, t: load((b - x) % 16, t) if (b - x) % 16 < count else zero
        )
        store(x, pltpu.roll(ring, (-C * x) % RING, 1) if x else ring)


def one_hot(size, column_of):
    row = lax.broadcasted_iota(jnp.int32, (size, size), 0)
    column = lax.broadcasted_iota(jnp.int32, (size, size), 1)
    return jnp.where(column == column_of(row), 1.0, 0.0).astype(BF16)


def dot(a, b):
    return jnp.dot(a, b, preferred_element_type=F32)


def kernel(
    in_hbm, cot_hbm, leg_hbm, filt_hbm, fwd_hbm, bwd_hbm,
    grad_out, filt_out,
    grid, leg, legp, filt, fwd, bwd, perm, permt, ring, xbuf, dbuf, strans, sback, coef, acc, gsum,
    zs_a, zs_b, zr_a, zr_b, ls_a, ls_b, lr_a, lr_b, gs, gr,
    load_sem, own_sem, zss, zrs, lss, lrs, gss, grs,
):
    lat, lon = lax.axis_index("lat"), lax.axis_index("lon")
    zs, zr, ls, lr = (zs_a, zs_b), (zr_a, zr_b), (ls_a, ls_b), (lr_a, lr_b)

    loads = [
        pltpu.make_async_copy(cot_hbm, grid.at[0], load_sem.at[0]),
        pltpu.make_async_copy(in_hbm, grid.at[1], load_sem.at[1]),
        pltpu.make_async_copy(leg_hbm, leg, load_sem.at[2]),
        pltpu.make_async_copy(fwd_hbm, fwd, load_sem.at[3]),
        pltpu.make_async_copy(bwd_hbm, bwd, load_sem.at[4]),
        pltpu.make_async_copy(filt_hbm, filt, load_sem.at[5]),
    ]
    for load in loads:
        load.start()
    barrier = pltpu.get_barrier_semaphore()

    def greet_lon(d, carry):
        pl.semaphore_signal(
            barrier, inc=1, device_id=(lat, lax.rem(lon + d, NZ)), device_id_type=MESH
        )
        return carry

    def greet_lat(d, carry):
        pl.semaphore_signal(
            barrier, inc=1, device_id=(lax.rem(lat + d, NL), lon), device_id_type=MESH
        )
        return carry

    lax.fori_loop(1, NZ, greet_lon, 0)
    lax.fori_loop(1, NL, greet_lat, 0)

    def send_lon(phase, p):
        def step(s, carry):
            half = lax.div(s + 1, 2)
            d = jnp.where(lax.rem(s, 2) == 0, 8 + half, 8 - half)
            to = lax.rem(lon + d, NZ)
            pltpu.make_async_remote_copy(
                src_ref=zs[p].at[phase, to],
                dst_ref=zr[p].at[phase, lon],
                send_sem=zss.at[phase, p],
                recv_sem=zrs.at[phase, p],
                device_id=(lat, to),
                device_id_type=MESH,
            ).start()
            return carry

        lax.fori_loop(0, NZ - 1, step, 0)
        own = pltpu.make_async_copy(zs[p].at[phase, lon], zr[p].at[phase, lon], own_sem.at[0])
        own.start()
        own.wait()

    def wait_lon(phase, p, sem):
        some = zr[p].at[phase, pl.ds(0, NZ - 1)]
        pltpu.make_async_copy(some, some, sem.at[phase, p]).wait()

    def send_lat(phase, p):
        def step(s, carry):
            to = lax.rem(lat + NL - 1 - s, NL)
            pltpu.make_async_remote_copy(
                src_ref=ls[p].at[phase, to],
                dst_ref=lr[p].at[phase, lat],
                send_sem=lss.at[phase, p],
                recv_sem=lrs.at[phase, p],
                device_id=(to, lon),
                device_id_type=MESH,
            ).start()
            return carry

        lax.fori_loop(0, NL - 1, step, 0)
        own = pltpu.make_async_copy(ls[p].at[phase, lat], lr[p].at[phase, lat], own_sem.at[1])
        own.start()
        own.wait()

    def wait_lat(phase, p, sem):
        some = lr[p].at[phase, pl.ds(0, NL - 1)]
        pltpu.make_async_copy(some, some, sem.at[phase, p]).wait()

    def pack(a, p):
        first, rows = PARTS[p]
        for i in range(16):
            if i < rows:
                wide = grid[a, first + i].astype(F32)
                ring[i] = pltpu.roll(wide, C * i, 1) if i else wide
            else:
                ring[i] = jnp.zeros((N, RING), F32)

        def one(z, carry):
            merged = merge_blocks(
                N, lambda b, t: ring[lax.rem(b + NZ - z, NZ), :, 128 * t : 128 * (t + 1)]
            )
            tiles = [jnp.zeros((16, 128), F32) for _ in range(TILES[p])]
            for g in range(GROUPS):
                base, shift = divmod(WIDTH[p] * g, 128)
                moved = pltpu.roll(
                    merged[16 * g : 16 * (g + 1)], lax.rem(shift + RING - C * z + RING, RING), 1
                )
                tiles[base] = tiles[base] + moved[:, :128]
                if base + 1 < TILES[p]:
                    tiles[base + 1] = tiles[base + 1] + moved[:, 128:256]
            zs[p][a, z] = jnp.concatenate(tiles, axis=1).astype(BF16)
            return carry

        lax.fori_loop(0, NZ, one, 0)

    def analyse_lon(a, p):
        width = WIDTH[p]
        wait_lon(a, p, zrs)
        for g in range(GROUPS):
            base, shift = divmod(width * g, 128)
            window = zr[p][a, :, :, 128 * base : 128 * base + 256].reshape(256, 256)
            if shift:
                window = pltpu.roll(window.astype(F32), 256 - shift, 1).astype(BF16)
            xbuf[pl.ds(256 * g, 256), :] = window
        for r in range(3):
            dbuf[pl.ds(256 * r, 256), :] = dot(fwd[pl.ds(256 * r, 256), :], xbuf[...])
        low = dbuf[pl.ds(0, 512), :128].reshape(NL, 16, 128)
        ls[p][a, :, :, :128] = low.astype(BF16)
        high = dbuf[pl.ds(512, 256), :128].reshape(NL, 8, 128)
        tail = width - 128
        if tail > 0:
            at = lax.broadcasted_iota(jnp.int32, (512, 128), 1)
            first = jnp.where(at < tail, dbuf[pl.ds(0, 512), 128:], 0.0).reshape(NL, 16, 128)
            last = jnp.where(at[:256] < tail, dbuf[pl.ds(512, 256), 128:], 0.0)
            ends = first[:, :8] + (
                pltpu.roll(first[:, 8:].reshape(256, 128), tail, 1)
                + pltpu.roll(last, 2 * tail, 1)
            ).reshape(NL, 8, 128)
        else:
            ends = jnp.zeros((NL, 8, 128), F32)
        ls[p][a, :, :, 128:] = jnp.concatenate([high, ends], axis=1).astype(BF16)
        send_lat(a, p)

    def gather_orders(a):
        for p in range(2):
            wait_lat(a, p, lrs)
            flat = lr[p][a].reshape(512, 256)
            dbuf[pl.ds(0, 512), :] = dot(perm[...], flat)
            at = lanes(NL)
            tail = WIDTH[p] - 128
            start = C * PARTS[p][0]
            for kk in range(2 * M):
                i, t = (kk, 0) if kk < 16 else (kk - 16, 1)
                main = dbuf[pl.ds(NL * i, NL), 128 * t : 128 * (t + 1)]
                zero = jnp.zeros((NL, 128), F32)
                if tail > 0:
                    part = kk // 8
                    end = dbuf[pl.ds(NL * (8 + kk % 8), NL), 128:]
                    end = pltpu.roll(end, (-tail * part) % 128, 1) if part else end
                    end = jnp.where(at < tail, end, zero)
                else:
                    end = zero
                    main = jnp.where(at < WIDTH[p], main, zero)
                wide = jnp.concatenate([main, end, zero], axis=1)
                shift = (start + C * (kk % M)) % RING
                wide = pltpu.roll(wide, shift, 1) if shift else wide
                if p == 0:
                    ring[kk // M * M + kk % M, :NL] = wide
                else:
                    ring[kk, :NL] = ring[kk, :NL] + wide

    def analyse_lat(a):
        gather_orders(a)
        for h in range(2):
            def load(i, t, h=h):
                return ring[M * h + i, :NL, 128 * t : 128 * (t + 1)]

            def store(x, value):
                xform[pl.ds(NL * x, NL), :] = value

            block_transpose(NL, Q, load, store)
            turned = jnp.transpose(xform[...])[: M * C]
            strans[pl.ds(M * C * h, M * C), :] = turned.astype(BF16)

    xform = gsum

    def scatter_orders():
        for h in range(2):
            half = sback[pl.ds(M * C * h, M * C), :]
            xform[pl.ds(0, M * C), :] = half
            turned = jnp.transpose(xform[...])
            at = lax.broadcasted_iota(jnp.int32, (NL, RING), 1)
            for q in range(Q):
                row = jnp.where(at < M * C, turned[NL * q : NL * (q + 1)], 0.0)
                ring[q, :NL] = pltpu.roll(row, C * q, 1) if q else row

            def load(i, t):
                return ring[i, :NL, 128 * t : 128 * (t + 1)]

            def store(x, value, h=h):
                ring[M + M * h + x, :NL] = value

            block_transpose(NL, Q, load, store)

    def synth_lat(p):
        at = lanes(NL)
        tail = WIDTH[p] - 128
        start = C * PARTS[p][0]
        zero = jnp.zeros((NL, 128), F32)

        def main(kk):
            if p == 0:
                return ring[M + kk, :NL, :128]
            moved = pltpu.roll(ring[M + kk, :NL], RING - start, 1)[:, :128]
            return jnp.where(at < WIDTH[p], moved, zero)

        def end(kk, part):
            value = jnp.where(at < tail, ring[M + kk, :NL, 128:256], zero)
            return pltpu.roll(value, tail * part, 1) if part else value

        for i in range(16):
            second = main(16 + i) if i < 8 else zero
            if i >= 8 and tail > 0:
                second = end(i - 8, 0) + end(i, 1) + end(i + 8, 2)
            both = jnp.concatenate([main(i), second], axis=1)
            xbuf[pl.ds(NL * i, NL), :] = both.astype(BF16)
        moved = dot(permt[...], xbuf[pl.ds(0, 512), :]).astype(BF16)
        ls[p][2] = moved.reshape(NL, 16, 256)
        send_lat(2, p)

    def synth_lon(p):
        width = WIDTH[p]
        tail = width - 128
        wait_lat(2, p, lrs)
        got = lr[p][2]
        xbuf[pl.ds(0, 512), :128] = got[:, :, :128].reshape(512, 128)
        second = got[:, :, 128:].astype(F32)
        xbuf[pl.ds(512, 256), :128] = second[:, :8].reshape(256, 128).astype(BF16)
        if tail > 0:
            ends = second[:, 8:].reshape(256, 128)
            one = pltpu.roll(ends, 128 - tail, 1)
            two = pltpu.roll(ends, 128 - 2 * tail, 1)
            both = jnp.concatenate([ends.reshape(NL, 8, 128), one.reshape(NL, 8, 128)], axis=1)
            xbuf[pl.ds(0, 512), 128:] = both.reshape(512, 128).astype(BF16)
            xbuf[pl.ds(512, 256), 128:] = two.astype(BF16)
        else:
            xbuf[:, 128:] = jnp.zeros((768, 128), BF16)
        at = lax.broadcasted_iota(jnp.int32, (256, 256), 1)
        tiles = [None] * TILES[p]
        for g in range(GROUPS):
            base, shift = divmod(width * g, 128)
            value = dot(bwd[pl.ds(256 * g, 256), :], xbuf[...])
            value = jnp.where(at < width, value, 0.0)
            value = pltpu.roll(value, shift, 1) if shift else value
            for t in range(2):
                if base + t < TILES[p]:
                    piece = value[:, 128 * t : 128 * (t + 1)]
                    old = tiles[base + t]
                    tiles[base + t] = piece if old is None else old + piece
        for t in range(TILES[p]):
            zs[p][2, :, :, 128 * t : 128 * (t + 1)] = tiles[t].astype(BF16).reshape(NZ, 16, 128)
        send_lon(2, p)

    def unpack(p):
        first, rows = PARTS[p]
        wait_lon(2, p, zrs)

        def one(z, carry):
            for g in range(GROUPS):
                base, shift = divmod(WIDTH[p] * g, 128)
                window = zr[p][2, z, :, 128 * base : 128 * base + 256].astype(F32)
                wide = jnp.concatenate([window, jnp.zeros((16, 128), F32)], axis=1)
                move = lax.rem(C * (z + first) + RING - shift, RING)
                ring[z, 16 * g : 16 * (g + 1), :] = pltpu.roll(wide, move, 1)
            return carry

        lax.fori_loop(0, NZ, one, 0)
        for q in range(first, first + rows):
            merged = merge_blocks(
                N, lambda b, t: ring[(b - q) % NZ, :, 128 * t : 128 * (t + 1)]
            )
            merged = pltpu.roll(merged, RING - C * q, 1) if q else merged
            grad_out[q] = merged.astype(BF16)

    loads[0].wait()
    for p in range(2):
        pack(0, p)
    pl.semaphore_wait(barrier, NZ - 1 + NL - 1)
    for p in range(2):
        send_lon(0, p)
    loads[1].wait()
    for p in range(2):
        pack(1, p)
        send_lon(1, p)

    perm[...] = one_hot(512, lambda r: (r & (NL - 1)) * 16 + (r >> 5))
    permt[...] = one_hot(512, lambda r: (r & 15) * NL + (r >> 4))
    order = one_hot(LATS, lambda r: (r & (NL - 1)) * Q + (r >> 5))
    loads[2].wait()

    def reorder(m, carry):
        legp[m] = dot(order, leg[m]).astype(BF16)
        return carry

    lax.fori_loop(0, M, reorder, 0)
    loads[5].wait()
    gain = []
    for r in range(2):
        wide = jnp.concatenate(
            [filt[:, r, :], jnp.zeros((DEGREES, 128 - C), F32)], axis=1
        )
        gain.append(jnp.transpose(wide)[:C])
    loads[3].wait()
    loads[4].wait()

    for p in range(2):
        analyse_lon(0, p)
    analyse_lat(0)

    def filter_order(m, carry):
        rows = pl.ds(pl.multiple_of(2 * C * m, 16), 2 * C)
        got = dot(strans[rows, :], legp[m])
        coef[m] = got
        re, im = got[:C], got[C:]
        back = jnp.concatenate(
            [gain[0] * re + gain[1] * im, gain[0] * im - gain[1] * re], axis=0
        ).astype(BF16)
        sback[rows, :] = lax.dot_general(
            back, legp[m], (((1,), (1,)), ((), ())), preferred_element_type=F32
        )
        return carry

    lax.fori_loop(0, M, filter_order, 0)
    scatter_orders()
    for p in range(2):
        synth_lat(p)
    for p in range(2):
        synth_lon(p)

    for p in range(2):
        analyse_lon(1, p)
    analyse_lat(1)
    acc[...] = jnp.zeros_like(acc)

    def correlate(m, carry):
        rows = pl.ds(pl.multiple_of(2 * C * m, 16), 2 * C)
        got = dot(strans[rows, :], legp[m])
        in_re, in_im = got[:C], got[C:]
        cot_re, cot_im = coef[m, :C], coef[m, C:]
        acc[pl.ds(0, C), :] += in_re * cot_re + in_im * cot_im
        acc[pl.ds(C, C), :] += in_re * cot_im - in_im * cot_re
        return carry

    lax.fori_loop(0, M, correlate, 0)
    gs[...] = jnp.transpose(acc[...])

    def send_sum(s, carry):
        to = lax.rem(lat + NL - 1 - s, NL)
        start = pl.multiple_of(Q * to - 4 * lax.rem(to, 2), 8)
        pltpu.make_async_remote_copy(
            src_ref=gs.at[pl.ds(start, 16)],
            dst_ref=gr.at[lat],
            send_sem=gss,
            recv_sem=grs,
            device_id=(to, lon),
            device_id_type=MESH,
        ).start()
        return carry

    lax.fori_loop(0, NL - 1, send_sum, 0)
    start = pl.multiple_of(Q * lat - 4 * lax.rem(lat, 2), 8)
    own = pltpu.make_async_copy(gs.at[pl.ds(start, 16)], gr.at[lat], own_sem.at[2])
    own.start()
    own.wait()
    some = gr.at[pl.ds(0, NL - 1)]
    pltpu.make_async_copy(some, some, grs).wait()
    total = jnp.sum(gr[...], axis=0)
    total = jnp.where(lax.rem(lat, 2) == 1, total[4:16], total[:12])
    filt_out[:, 0, :] = total[:, :C]
    filt_out[:, 1, :] = total[:, C : 2 * C]

    for p in range(2):
        unpack(p)

    for phase in range(3):
        for p in range(2):
            wait_lon(phase, p, zss)
            wait_lat(phase, p, lss)
    pltpu.make_async_copy(some, some, gss).wait()


def local(grid_in, grid_cot, legendre, filters):
    fwd, bwd = fourier_tables()
    vmem = pltpu.VMEM
    any_space = pl.BlockSpec(memory_space=pl.ANY)
    return pl.pallas_call(
        kernel,
        out_shape=(
            jax.ShapeDtypeStruct((Q, N, CHANNELS), BF16),
            jax.ShapeDtypeStruct((Q, 2, C), F32),
        ),
        in_specs=[any_space] * 6,
        out_specs=(pl.BlockSpec(memory_space=vmem), pl.BlockSpec(memory_space=vmem)),
        scratch_shapes=[
            vmem((2, Q, N, CHANNELS), BF16),
            vmem((M, LATS, DEGREES), BF16),
            vmem((M, LATS, DEGREES), BF16),
            vmem((DEGREES, 2, C), F32),
            vmem((2 * DEGREES, LONS), BF16),
            vmem((LONS, 2 * DEGREES), BF16),
            vmem((512, 512), BF16),
            vmem((512, 512), BF16),
            vmem((3 * M, N, RING), F32),
            vmem((768, 256), BF16),
            vmem((768, 256), F32),
            vmem((2 * M * C, LATS), BF16),
            vmem((2 * M * C, LATS), F32),
            vmem((M, 2 * C, DEGREES), F32),
            vmem((128, DEGREES), F32),
            vmem((RING, LATS), F32),
            vmem((3, NZ, 16, 128 * TILES[0]), BF16),
            vmem((3, NZ, 16, 128 * TILES[1]), BF16),
            vmem((3, NZ, 16, 128 * TILES[0]), BF16),
            vmem((3, NZ, 16, 128 * TILES[1]), BF16),
            vmem((3, NL, 16, 256), BF16),
            vmem((3, NL, 16, 256), BF16),
            vmem((3, NL, 16, 256), BF16),
            vmem((3, NL, 16, 256), BF16),
            vmem((DEGREES, 128), F32),
            vmem((NL, 16, 128), F32),
            pltpu.SemaphoreType.DMA((6,)),
            pltpu.SemaphoreType.DMA((3,)),
            pltpu.SemaphoreType.DMA((3, 2)),
            pltpu.SemaphoreType.DMA((3, 2)),
            pltpu.SemaphoreType.DMA((3, 2)),
            pltpu.SemaphoreType.DMA((3, 2)),
            pltpu.SemaphoreType.DMA,
            pltpu.SemaphoreType.DMA,
        ],
        compiler_params=pltpu.CompilerParams(
            collective_id=0, has_side_effects=True, vmem_limit_bytes=56 * 1024 * 1024
        ),
    )(grid_in, grid_cot, legendre, filters, jnp.asarray(fwd), jnp.asarray(bwd))


def solution(mesh):
    return jax.shard_map(
        local,
        mesh=mesh,
        in_specs=(
            P("lat", "lon", None),
            P("lat", "lon", None),
            P("lat", None, None),
            P(None, None, "lon"),
        ),
        out_specs=(P("lat", "lon", None), P("lat", None, "lon")),
        check_vma=False,
    )
```

```python
import math

import jax
import jax.numpy as jnp
import ml_dtypes
import numpy as np
from jax import lax
from jax.experimental import pallas as pl
from jax.experimental.pallas import tpu as pltpu
from jax.sharding import PartitionSpec as P

MESH = pl.DeviceIdType.MESH
BF16 = jnp.bfloat16
F32 = jnp.float32

NZ, NL = 16, 32
LATS, LONS, DEGREES, CHANNELS = 384, 768, 384, 384
Q, N, C = LATS // NL, LONS // NZ, CHANNELS // NZ
M = DEGREES // NL
K = 2 * M
RING = 384
GROUPS = N // 16
SLOT = 16

PARTS = ((0, 14), (14, 10))
WIDTH = tuple(Q * count for _, count in PARTS)
TILES = tuple(-(-GROUPS * w // 128) for w in WIDTH)


def fourier_tables():
    points = np.arange(LONS, dtype=np.int64)[:, None]
    order = np.arange(DEGREES, dtype=np.int64)[None, :]
    phases = (points * order) % LONS
    angles = phases.astype(np.float32) * np.float32(2.0 * math.pi / LONS)
    pair = np.stack([np.cos(angles), -np.sin(angles)], axis=2) * np.float32(LONS ** (-0.5))
    table = pair.reshape(LONS, 2 * DEGREES).astype(ml_dtypes.bfloat16)
    n_of = np.arange(LONS).reshape(NZ, GROUPS, 16).transpose(1, 0, 2).reshape(-1)
    k = np.arange(2 * DEGREES).reshape(NL, 2 * M)
    k_of = np.concatenate([k[:, :16].reshape(-1), k[:, 16:].reshape(-1)])
    back = table[n_of][:, k_of]
    return np.ascontiguousarray(back.T), np.ascontiguousarray(back)


def lanes(rows):
    return lax.broadcasted_iota(jnp.int32, (rows, 128), 1)


def merge(rows, start, step, count, pick):
    at = lanes(rows)
    tiles = []
    for t in range(start // 128, (start + step * count - 1) // 128 + 1):
        value = None
        for i in range(count):
            low, high = start + step * i - 128 * t, start + step * (i + 1) - 128 * t
            if high <= 0 or low >= 128:
                continue
            block = pick(i, t)
            value = block if value is None else jnp.where(at >= low, block, value)
        tiles.append(value)
    return tiles


def shift_left(tiles, shift):
    wide = jnp.concatenate(tiles, axis=1) if len(tiles) > 1 else tiles[0]
    size = 128 * len(tiles)
    return pltpu.roll(wide, (size - shift) % size, 1) if shift % size else wide


def one_hot(size, column_of):
    row = lax.broadcasted_iota(jnp.int32, (size, size), 0)
    column = lax.broadcasted_iota(jnp.int32, (size, size), 1)
    return jnp.where(column == column_of(row), 1.0, 0.0).astype(BF16)


def dot(a, b):
    return jnp.dot(a, b, preferred_element_type=F32)


def kernel(
    in_hbm, cot_hbm, leg_hbm, filt_hbm, fwd_hbm, bwd_hbm,
    grad_out, filt_out,
    grid, leg, legp, filt, fwd, bwd, perm, permt, ring, pbuf, gain, xbuf, dbuf, xform, strans, sback, coef, acc,
    zs_a, zs_b, zr_a, zr_b, ls_a, ls_b, lr_a, lr_b, gs, gr,
    load_sem, own_sem, zss, zrs, lss, lrs, gss, grs,
):
    lat, lon = lax.axis_index("lat"), lax.axis_index("lon")
    zs, zr, ls, lr = (zs_a, zs_b), (zr_a, zr_b), (ls_a, ls_b), (lr_a, lr_b)

    barrier = pltpu.get_barrier_semaphore()
    for d in (8, 7, 9, 6, 10, 5, 11, 4, 12, 3, 13, 2, 14, 1, 15):
        pl.semaphore_signal(
            barrier, inc=1, device_id=(lat, lax.rem(lon + d, NZ)), device_id_type=MESH
        )

    def greet(d, carry):
        pl.semaphore_signal(
            barrier, inc=1, device_id=(lax.rem(lat + d, NL), lon), device_id_type=MESH
        )
        return carry

    lax.fori_loop(1, NL, greet, 0)
    loads = [
        pltpu.make_async_copy(cot_hbm, grid.at[0], load_sem.at[0]),
        pltpu.make_async_copy(in_hbm, grid.at[1], load_sem.at[1]),
        pltpu.make_async_copy(leg_hbm, leg, load_sem.at[2]),
        pltpu.make_async_copy(fwd_hbm, fwd, load_sem.at[3]),
        pltpu.make_async_copy(bwd_hbm, bwd, load_sem.at[4]),
        pltpu.make_async_copy(filt_hbm, filt, load_sem.at[5]),
    ]
    for load in loads:
        load.start()
    def send_lon(phase, p):
        def step(s, carry):
            half = lax.div(s + 1, 2)
            d = jnp.where(lax.rem(s, 2) == 0, 8 + half, 8 - half)
            to = lax.rem(lon + d, NZ)
            pltpu.make_async_remote_copy(
                src_ref=zs[p].at[phase, to],
                dst_ref=zr[p].at[phase, lon],
                send_sem=zss.at[phase, p],
                recv_sem=zrs.at[phase, p],
                device_id=(lat, to),
                device_id_type=MESH,
            ).start()
            return carry

        lax.fori_loop(0, NZ - 1, step, 0)
        zr[p][phase, lon] = zs[p][phase, lon]

    def wait_lon(phase, p, sem):
        some = zr[p].at[phase, pl.ds(0, NZ - 1)]
        pltpu.make_async_copy(some, some, sem.at[phase, p]).wait()

    def send_lat(phase, p):
        def step(s, carry):
            to = lat ^ (NL - 1 - s)
            pltpu.make_async_remote_copy(
                src_ref=ls[p].at[phase, to],
                dst_ref=lr[p].at[phase, lat],
                send_sem=lss.at[phase, p],
                recv_sem=lrs.at[phase, p],
                device_id=(to, lon),
                device_id_type=MESH,
            ).start()
            return carry

        lax.fori_loop(0, NL - 1, step, 0)
        lr[p][phase, lat] = ls[p][phase, lat]

    def wait_lat(phase, p, sem):
        some = lr[p].at[phase, pl.ds(0, NL - 1)]
        pltpu.make_async_copy(some, some, sem.at[phase, p]).wait()

    def pack(a, p):
        first, count = PARTS[p]
        at = lanes(16)
        for q in range(Q):
            wide = grid[a, q]
            pbuf[q] = pltpu.roll(wide, count * q, 1) if q else wide
        for z in range(NZ):
            start = C * z + first
            moved = jnp.concatenate(
                merge(N, start, count, Q, lambda q, t: pbuf[q, :, 128 * (t % 3) : 128 * (t % 3) + 128]),
                axis=1,
            )
            size = moved.shape[1]
            if size == 128:
                moved = jnp.concatenate([moved, moved], axis=1)
                size = 256
            tiles = [None] * (TILES[p] + 1)
            for g in range(GROUPS):
                base, shift = divmod(WIDTH[p] * g, 128)
                turn = (shift - start % 128) % size
                rows = moved[16 * g : 16 * (g + 1)]
                rows = pltpu.roll(rows, turn, 1) if turn else rows
                old = tiles[base]
                tiles[base] = rows[:, :128] if old is None else jnp.where(at >= shift, rows[:, :128], old)
                tiles[base + 1] = rows[:, 128:256]
            zs[p][a, z] = jnp.concatenate(tiles[: TILES[p]], axis=1)

    def analyse_lon(a, p):
        width = WIDTH[p]
        wait_lon(a, p, zrs)
        for g in range(GROUPS):
            base, shift = divmod(width * g, 128)
            window = zr[p][a, :, :, 128 * base : 128 * base + 256].reshape(256, 256)
            if shift:
                window = pltpu.roll(window.astype(F32), 256 - shift, 1).astype(BF16)
            xbuf[pl.ds(256 * g, 256), :] = window
        for r in range(3):
            dbuf[pl.ds(256 * r, 256), :] = dot(fwd[pl.ds(256 * r, 256), :], xbuf[...])
        low = dbuf[pl.ds(0, 512), :128].reshape(NL, 16, 128)
        ls[p][a, :, :, :128] = low.astype(BF16)
        high = dbuf[pl.ds(512, 256), :128].reshape(NL, 8, 128)
        tail = width - 128
        if tail > 0:
            at = lax.broadcasted_iota(jnp.int32, (512, 128), 1)
            first = jnp.where(at < tail, dbuf[pl.ds(0, 512), 128:], 0.0).reshape(NL, 16, 128)
            last = jnp.where(at[:256] < tail, dbuf[pl.ds(512, 256), 128:], 0.0)
            ends = first[:, :8] + (
                pltpu.roll(first[:, 8:].reshape(256, 128), tail, 1)
                + pltpu.roll(last, 2 * tail, 1)
            ).reshape(NL, 8, 128)
        else:
            ends = jnp.zeros((NL, 8, 128), F32)
        ls[p][a, :, :, 128:] = jnp.concatenate([high, ends], axis=1).astype(BF16)
        send_lat(a, p)

    def analyse_lat(a, p):
        count = PARTS[p][1]
        tail = WIDTH[p] - 128
        at = lanes(NL)
        wait_lat(a, p, lrs)
        dbuf[pl.ds(0, 512), :] = dot(perm[...], lr[p][a].reshape(512, 256))
        for kk in range(K):
            base, shift = divmod(SLOT * kk, 128)
            i, t = (kk, 0) if kk < 16 else (kk - 16, 1)
            main = dbuf[pl.ds(NL * i, NL), 128 * t : 128 * (t + 1)]
            main = pltpu.roll(main, shift, 1) if shift else main
            ring[kk, :, :128] = main
            if tail > 0:
                end = dbuf[pl.ds(NL * (8 + kk % 8), NL), 128:]
                turn = (shift - tail * (kk // 8)) % 128
                end = pltpu.roll(end, turn, 1) if turn else end
                ring[kk, :, 128:256] = jnp.where(at < shift, main, end) if shift else end
                ring[kk, :, 256:384] = end
            else:
                ring[kk, :, 128:256] = main
        for q in range(Q):
            start = count * q

            def pick(kk, t):
                t -= SLOT * kk // 128
                return ring[kk, :, 128 * t : 128 * (t + 1)]

            tiles = merge(NL, start, SLOT, K, pick)
            xform[pl.ds(NL * q, NL), :] = shift_left(tiles, start % 128)[:, : SLOT * K]
        strans[...] = jnp.transpose(xform[...]).astype(BF16)

    def synth_lat(p):
        count = PARTS[p][1]
        tail = WIDTH[p] - 128
        at = lanes(NL)
        xform[...] = jnp.transpose(sback[...])
        blank = jnp.zeros((NL, 128), F32)
        for q in range(Q):
            row = jnp.concatenate([xform[pl.ds(NL * q, NL), :], blank], axis=1)
            shift = count * q % 128
            ring[q] = pltpu.roll(row, shift, 1) if shift else row

        def column(kk):
            def pick(q, t):
                t -= count * q // 128
                return ring[q, :, 128 * t : 128 * (t + 1)]

            tiles = merge(NL, SLOT * kk, count, Q, pick)
            return shift_left(tiles, SLOT * kk % 128)

        for i in range(16):
            low = column(i)
            ring[Q + i % 8, :, 128 * (i // 8) : 128 * (i // 8 + 1)] = low[:, :128]
            if tail > 0:
                done = low[:, 128:256]
                if i < 8:
                    ring[Q + i, :, 256:384] = done
                else:
                    old = ring[Q + i - 8, :, 256:384]
                    ring[Q + i - 8, :, 256:384] = jnp.where(at >= tail, pltpu.roll(done, tail, 1), old)
        for i in range(8):
            high = column(16 + i)
            low = ring[Q + i, :, :128]
            xbuf[pl.ds(NL * i, NL), :] = jnp.concatenate([low, high[:, :128]], axis=1).astype(BF16)
            ends = blank
            if tail > 0:
                ends = jnp.where(
                    at >= 2 * tail, pltpu.roll(high[:, 128:256], 2 * tail, 1), ring[Q + i, :, 256:384]
                )
            low = ring[Q + i, :, 128:256]
            xbuf[pl.ds(NL * (8 + i), NL), :] = jnp.concatenate([low, ends], axis=1).astype(BF16)
        moved = dot(permt[...], xbuf[pl.ds(0, 512), :]).astype(BF16)
        ls[p][2] = moved.reshape(NL, 16, 256)
        send_lat(2, p)

    def synth_lon(p):
        width = WIDTH[p]
        tail = width - 128
        wait_lat(2, p, lrs)
        got = lr[p][2]
        xbuf[pl.ds(0, 512), :128] = got[:, :, :128].reshape(512, 128)
        second = got[:, :, 128:].astype(F32)
        xbuf[pl.ds(512, 256), :128] = second[:, :8].reshape(256, 128).astype(BF16)
        if tail > 0:
            ends = second[:, 8:].reshape(256, 128)
            one = pltpu.roll(ends, 128 - tail, 1)
            two = pltpu.roll(ends, 128 - 2 * tail, 1)
            both = jnp.concatenate([ends.reshape(NL, 8, 128), one.reshape(NL, 8, 128)], axis=1)
            xbuf[pl.ds(0, 512), 128:] = both.reshape(512, 128).astype(BF16)
            xbuf[pl.ds(512, 256), 128:] = two.astype(BF16)
        else:
            xbuf[:, 128:] = jnp.zeros((768, 128), BF16)
        at = lax.broadcasted_iota(jnp.int32, (256, 256), 1)
        tiles = [None] * TILES[p]
        for g in range(GROUPS):
            base, shift = divmod(width * g, 128)
            value = dot(bwd[pl.ds(256 * g, 256), :], xbuf[...])
            value = jnp.where(at < width, value, 0.0)
            value = pltpu.roll(value, shift, 1) if shift else value
            for t in range(2):
                if base + t < TILES[p]:
                    piece = value[:, 128 * t : 128 * (t + 1)]
                    old = tiles[base + t]
                    tiles[base + t] = piece if old is None else old + piece
        for t in range(TILES[p]):
            zs[p][2, :, :, 128 * t : 128 * (t + 1)] = tiles[t].astype(BF16).reshape(NZ, 16, 128)
        send_lon(2, p)

    def unpack(p):
        first, count = PARTS[p]
        wait_lon(2, p, zrs)
        for z in range(NZ):
            for g in range(GROUPS):
                base, shift = divmod(WIDTH[p] * g, 128)
                window = [zr[p][2, z, :, 128 * t : 128 * (t + 1)] for t in range(base, min(base + 2, TILES[p]))]
                window += [window[-1]] * (3 - len(window))
                turn = (C * z + first - shift) % RING
                wide = jnp.concatenate(window, axis=1)
                pbuf[z, 16 * g : 16 * (g + 1), :] = pltpu.roll(wide, turn, 1) if turn else wide
        at = lanes(N)
        for q in range(Q):
            start = first + count * q
            tiles = []
            for t in range(3):
                low = 128 * t - start
                z = low // C
                value = pbuf[z % NZ, :, 128 * t : 128 * (t + 1)]
                while C * (z + 1) - low < 128:
                    z += 1
                    value = jnp.where(
                        at >= C * z - low, pbuf[z % NZ, :, 128 * t : 128 * (t + 1)], value
                    )
                tiles.append(value)
            whole = shift_left(tiles, count * q)
            if p == 0:
                grad_out[q] = whole
            else:
                for t in range(3):
                    span = slice(128 * t, 128 * (t + 1))
                    inner = lax.rem(at + 128 * t, C)
                    grad_out[q, :, span] = jnp.where(inner < first, grad_out[q, :, span], whole[:, span])

    loads[0].wait()
    pack(0, 0)
    pl.semaphore_wait(barrier, NZ - 1 + NL - 1)
    send_lon(0, 0)
    pack(0, 1)
    send_lon(0, 1)
    loads[1].wait()
    pack(1, 0)
    send_lon(1, 0)
    pack(1, 1)
    send_lon(1, 1)

    perm[...] = one_hot(512, lambda r: (r & (NL - 1)) * 16 + (r >> 5))
    permt[...] = one_hot(512, lambda r: (r & 15) * NL + (r >> 4))
    order = one_hot(LATS, lambda r: (r & (NL - 1)) * Q + (r >> 5))
    loads[2].wait()

    def reorder(m, carry):
        legp[m] = dot(order, leg[m]).astype(BF16)
        return carry

    lax.fori_loop(0, M, reorder, 0, unroll=2)
    loads[5].wait()
    gain[0] = filt[:, :SLOT]
    for r in range(2):
        first, count = PARTS[1]
        gain[1, r, :count] = filt[r, first:]
        gain[1, r, count:] = jnp.zeros((SLOT - count, DEGREES), F32)
    loads[3].wait()
    loads[4].wait()

    def spectrum(m):
        rows = pl.ds(pl.multiple_of(2 * SLOT * m, 2 * SLOT), 2 * SLOT)
        return dot(strans[rows, :], legp[m])

    def filter_cot(p):
        def analyse(m, carry):
            coef[p, m] = spectrum(m)
            return carry

        lax.fori_loop(0, M, analyse, 0, unroll=4)

        def synth(m, carry):
            re, im = coef[p, m, :SLOT], coef[p, m, SLOT:]
            back = jnp.concatenate(
                [gain[p, 0] * re + gain[p, 1] * im, gain[p, 0] * im - gain[p, 1] * re], axis=0
            ).astype(BF16)
            rows = pl.ds(pl.multiple_of(2 * SLOT * m, 2 * SLOT), 2 * SLOT)
            sback[rows, :] = lax.dot_general(
                back, legp[m], (((1,), (1,)), ((), ())), preferred_element_type=F32
            )
            return carry

        lax.fori_loop(0, M, synth, 0, unroll=4)

    def correlate(p):
        def one(m, carry):
            got = spectrum(m)
            in_re, in_im = got[:SLOT], got[SLOT:]
            cot_re, cot_im = coef[p, m, :SLOT], coef[p, m, SLOT:]
            acc[pl.ds(2 * SLOT * p, SLOT), :] += in_re * cot_re + in_im * cot_im
            acc[pl.ds(2 * SLOT * p + SLOT, SLOT), :] += in_re * cot_im - in_im * cot_re
            return carry

        lax.fori_loop(0, M, one, 0, unroll=4)

    acc[...] = jnp.zeros_like(acc)
    analyse_lon(0, 0)
    analyse_lat(0, 0)
    analyse_lon(0, 1)
    filter_cot(0)
    synth_lat(0)
    analyse_lat(0, 1)
    filter_cot(1)
    synth_lat(1)
    synth_lon(0)
    analyse_lon(1, 0)
    synth_lon(1)
    analyse_lon(1, 1)
    analyse_lat(1, 0)
    correlate(0)
    analyse_lat(1, 1)
    correlate(1)
    gs[...] = jnp.transpose(acc[...])

    def send_sum(s, carry):
        to = lat ^ (NL - 1 - s)
        start = pl.multiple_of(Q * to - 4 * lax.rem(to, 2), 8)
        pltpu.make_async_remote_copy(
            src_ref=gs.at[pl.ds(start, 16)],
            dst_ref=gr.at[lat],
            send_sem=gss,
            recv_sem=grs,
            device_id=(to, lon),
            device_id_type=MESH,
        ).start()
        return carry

    lax.fori_loop(0, NL - 1, send_sum, 0)
    start = pl.multiple_of(Q * lat - 4 * lax.rem(lat, 2), 8)
    own = pltpu.make_async_copy(gs.at[pl.ds(start, 16)], gr.at[lat], own_sem.at[0])
    own.start()
    own.wait()
    some = gr.at[pl.ds(0, NL - 1)]
    unpack(0)
    pltpu.make_async_copy(some, some, grs).wait()
    total = jnp.sum(gr[...], axis=0)
    total = jnp.where(lax.rem(lat, 2) == 1, total[4:16], total[:12])
    for r in range(2):
        for p in range(2):
            first, count = PARTS[p]
            low = 2 * SLOT * p + SLOT * r
            filt_out[:, r, first : first + count] = total[:, low : low + count]
    unpack(1)

    for phase in range(3):
        for p in range(2):
            wait_lon(phase, p, zss)
            wait_lat(phase, p, lss)
    pltpu.make_async_copy(some, some, gss).wait()


def hand_over(grad_in, filt_in, grad_out, filt_out):
    grad_out[...] = grad_in[...]
    filt_out[...] = filt_in[...]


def local(grid_in, grid_cot, legendre, filters):
    fwd, bwd = fourier_tables()
    vmem = pltpu.VMEM
    any_space = pl.BlockSpec(memory_space=pl.ANY)
    outs = pl.pallas_call(
        kernel,
        out_shape=(
            jax.ShapeDtypeStruct((Q, N, CHANNELS), BF16),
            jax.ShapeDtypeStruct((Q, 2, C), F32),
        ),
        in_specs=[any_space] * 6,
        out_specs=(pl.BlockSpec(memory_space=vmem), pl.BlockSpec(memory_space=vmem)),
        scratch_shapes=[
            vmem((2, Q, N, CHANNELS), BF16),
            vmem((M, LATS, DEGREES), BF16),
            vmem((M, LATS, DEGREES), BF16),
            vmem((2, C, DEGREES), F32),
            vmem((2 * DEGREES, LONS), BF16),
            vmem((LONS, 2 * DEGREES), BF16),
            vmem((512, 512), BF16),
            vmem((512, 512), BF16),
            vmem((K, NL, 512), F32),
            vmem((NZ, N, RING), BF16),
            vmem((2, 2, SLOT, DEGREES), F32),
            vmem((768, 256), BF16),
            vmem((768, 256), F32),
            vmem((LATS, SLOT * K), F32),
            vmem((SLOT * K, LATS), BF16),
            vmem((SLOT * K, LATS), F32),
            vmem((2, M, 2 * SLOT, DEGREES), F32),
            vmem((128, DEGREES), F32),
            vmem((3, NZ, 16, 128 * TILES[0]), BF16),
            vmem((3, NZ, 16, 128 * TILES[1]), BF16),
            vmem((3, NZ, 16, 128 * TILES[0]), BF16),
            vmem((3, NZ, 16, 128 * TILES[1]), BF16),
            vmem((3, NL, 16, 256), BF16),
            vmem((3, NL, 16, 256), BF16),
            vmem((3, NL, 16, 256), BF16),
            vmem((3, NL, 16, 256), BF16),
            vmem((DEGREES, 128), F32),
            vmem((NL, 16, 128), F32),
            pltpu.SemaphoreType.DMA((6,)),
            pltpu.SemaphoreType.DMA((1,)),
            pltpu.SemaphoreType.DMA((3, 2)),
            pltpu.SemaphoreType.DMA((3, 2)),
            pltpu.SemaphoreType.DMA((3, 2)),
            pltpu.SemaphoreType.DMA((3, 2)),
            pltpu.SemaphoreType.DMA,
            pltpu.SemaphoreType.DMA,
        ],
        compiler_params=pltpu.CompilerParams(
            collective_id=0, has_side_effects=True, vmem_limit_bytes=56 * 1024 * 1024
        ),
    )(
        grid_in, grid_cot, legendre, jnp.transpose(filters, (1, 2, 0)), jnp.asarray(fwd), jnp.asarray(bwd)
    )
    return pl.pallas_call(
        hand_over,
        out_shape=tuple(jax.ShapeDtypeStruct(out.shape, out.dtype) for out in outs),
        in_specs=[pl.BlockSpec(memory_space=vmem)] * 2,
        out_specs=(pl.BlockSpec(memory_space=vmem), pl.BlockSpec(memory_space=vmem)),
    )(*outs)


def solution(mesh):
    return jax.shard_map(
        local,
        mesh=mesh,
        in_specs=(
            P("lat", "lon", None),
            P("lat", "lon", None),
            P("lat", None, None),
            P(None, None, "lon"),
        ),
        out_specs=(P("lat", "lon", None), P("lat", None, "lon")),
        check_vma=False,
    )
```

```python
import math

import jax
import jax.numpy as jnp
import ml_dtypes
import numpy as np
from jax import lax
from jax.experimental import pallas as pl
from jax.experimental.pallas import tpu as pltpu
from jax.sharding import PartitionSpec as P

MESH = pl.DeviceIdType.MESH
BF16 = jnp.bfloat16
F32 = jnp.float32

NZ, NL = 16, 32
LATS, LONS, DEGREES, CHANNELS = 384, 768, 384, 384
Q, N, C = LATS // NL, LONS // NZ, CHANNELS // NZ
M = DEGREES // NL
K = 2 * M
RING = 384
GROUPS = N // 16
SLOT = 16

PARTS = ((0, 14), (14, 10))
WIDTH = tuple(Q * count for _, count in PARTS)
TILES = tuple(-(-GROUPS * w // 128) for w in WIDTH)


def fourier_tables():
    points = np.arange(LONS, dtype=np.int64)[:, None]
    order = np.arange(DEGREES, dtype=np.int64)[None, :]
    phases = (points * order) % LONS
    angles = phases.astype(np.float32) * np.float32(2.0 * math.pi / LONS)
    pair = np.stack([np.cos(angles), -np.sin(angles)], axis=2) * np.float32(LONS ** (-0.5))
    table = pair.reshape(LONS, 2 * DEGREES).astype(ml_dtypes.bfloat16)
    n_of = np.arange(LONS).reshape(NZ, GROUPS, 16).transpose(1, 0, 2).reshape(-1)
    k = np.arange(2 * DEGREES).reshape(NL, 2 * M)
    k_of = np.concatenate([k[:, :16].reshape(-1), k[:, 16:].reshape(-1)])
    back = table[n_of][:, k_of]
    return np.ascontiguousarray(back.T), np.ascontiguousarray(back)


def lanes(rows):
    return lax.broadcasted_iota(jnp.int32, (rows, 128), 1)


def merge(rows, start, step, count, pick):
    at = lanes(rows)
    tiles = []
    for t in range(start // 128, (start + step * count - 1) // 128 + 1):
        value = None
        for i in range(count):
            low, high = start + step * i - 128 * t, start + step * (i + 1) - 128 * t
            if high <= 0 or low >= 128:
                continue
            block = pick(i, t)
            value = block if value is None else jnp.where(at >= low, block, value)
        tiles.append(value)
    return tiles


def shift_left(tiles, shift):
    wide = jnp.concatenate(tiles, axis=1) if len(tiles) > 1 else tiles[0]
    size = 128 * len(tiles)
    return pltpu.roll(wide, (size - shift) % size, 1) if shift % size else wide


def one_hot(size, column_of):
    row = lax.broadcasted_iota(jnp.int32, (size, size), 0)
    column = lax.broadcasted_iota(jnp.int32, (size, size), 1)
    return jnp.where(column == column_of(row), 1.0, 0.0).astype(BF16)


def dot(a, b):
    return jnp.dot(a, b, preferred_element_type=F32)


def kernel(
    in_hbm, cot_hbm, leg_hbm, filt_hbm, fwd_hbm, bwd_hbm,
    grad_out, filt_out,
    grid, leg, legp, filt, fwd, bwd, perm, permt, ring, pbuf, gain, xbuf, dbuf, xform, strans, sback, coef, acc,
    zs_a, zs_b, zr_a, zr_b, ls_a, ls_b, lr_a, lr_b, gs, gr,
    load_sem, own_sem, zss, zrs, lss, lrs, gss, grs, far_sem, col_sem,
):
    lat, lon = lax.axis_index("lat"), lax.axis_index("lon")
    zs, zr, ls, lr = (zs_a, zs_b), (zr_a, zr_b), (ls_a, ls_b), (lr_a, lr_b)

    def ring_peer(d):
        return (lat, lax.rem(lon + d, NZ))

    def row_peer(d):
        return ((lat & 6) | ((lat ^ d) & 25), lon)

    def column_peer(d):
        return ((lat & 25) | ((lat + 2 * d) & 6), lon)

    barrier = pltpu.get_barrier_semaphore()
    near = (4, 12, 3, 13, 2, 14, 1, 15)
    far = (8, 7, 9, 6, 10, 5, 11)
    greeted = [ring_peer(d) for d in near]
    greeted += [row_peer(d) for d in (25, 24, 17, 16, 9, 8, 1)]
    greeted += [column_peer(d) for d in (2, 1, 3)]
    for peer in greeted:
        pl.semaphore_signal(barrier, inc=1, device_id=peer, device_id_type=MESH)
    loads = [
        pltpu.make_async_copy(cot_hbm, grid.at[0], load_sem.at[0]),
        pltpu.make_async_copy(in_hbm, grid.at[1], load_sem.at[1]),
        pltpu.make_async_copy(leg_hbm, leg, load_sem.at[2]),
        pltpu.make_async_copy(fwd_hbm, fwd, load_sem.at[3]),
        pltpu.make_async_copy(bwd_hbm, bwd, load_sem.at[4]),
        pltpu.make_async_copy(filt_hbm, filt, load_sem.at[5]),
    ]
    for load in loads:
        load.start()
    def send_lon(phase, p, distances=far + near, own=True):
        for d in distances:
            to = lax.rem(lon + d, NZ)
            pltpu.make_async_remote_copy(
                src_ref=zs[p].at[phase, to],
                dst_ref=zr[p].at[phase, lon],
                send_sem=zss.at[phase, p],
                recv_sem=zrs.at[phase, p],
                device_id=(lat, to),
                device_id_type=MESH,
            ).start()
        if own:
            zr[p][phase, lon] = zs[p][phase, lon]

    def wait_lon(phase, p, sem):
        some = zr[p].at[phase, pl.ds(0, NZ - 1)]
        pltpu.make_async_copy(some, some, sem.at[phase, p]).wait()

    def send_lat(phase, p):
        def step(s, carry):
            to = lat ^ (NL - 1 - s)
            pltpu.make_async_remote_copy(
                src_ref=ls[p].at[phase, to],
                dst_ref=lr[p].at[phase, lat],
                send_sem=lss.at[phase, p],
                recv_sem=lrs.at[phase, p],
                device_id=(to, lon),
                device_id_type=MESH,
            ).start()
            return carry

        lax.fori_loop(0, NL - 1, step, 0)
        lr[p][phase, lat] = ls[p][phase, lat]

    def wait_lat(phase, p, sem):
        some = lr[p].at[phase, pl.ds(0, NL - 1)]
        pltpu.make_async_copy(some, some, sem.at[phase, p]).wait()

    def pack(a, p):
        first, count = PARTS[p]
        at = lanes(16)
        for q in range(Q):
            wide = grid[a, q]
            pbuf[q] = pltpu.roll(wide, count * q, 1) if q else wide
        for z in range(NZ):
            start = C * z + first
            moved = jnp.concatenate(
                merge(N, start, count, Q, lambda q, t: pbuf[q, :, 128 * (t % 3) : 128 * (t % 3) + 128]),
                axis=1,
            )
            size = moved.shape[1]
            if size == 128:
                moved = jnp.concatenate([moved, moved], axis=1)
                size = 256
            tiles = [None] * (TILES[p] + 1)
            for g in range(GROUPS):
                base, shift = divmod(WIDTH[p] * g, 128)
                turn = (shift - start % 128) % size
                rows = moved[16 * g : 16 * (g + 1)]
                rows = pltpu.roll(rows, turn, 1) if turn else rows
                old = tiles[base]
                tiles[base] = rows[:, :128] if old is None else jnp.where(at >= shift, rows[:, :128], old)
                tiles[base + 1] = rows[:, 128:256]
            zs[p][a, z] = jnp.concatenate(tiles[: TILES[p]], axis=1)

    def analyse_lon(a, p):
        width = WIDTH[p]
        wait_lon(a, p, zrs)
        for g in range(GROUPS):
            base, shift = divmod(width * g, 128)
            window = zr[p][a, :, :, 128 * base : 128 * base + 256].reshape(256, 256)
            if shift:
                window = pltpu.roll(window.astype(F32), 256 - shift, 1).astype(BF16)
            xbuf[pl.ds(256 * g, 256), :] = window
        for r in range(3):
            dbuf[pl.ds(256 * r, 256), :] = dot(fwd[pl.ds(256 * r, 256), :], xbuf[...])
        low = dbuf[pl.ds(0, 512), :128].reshape(NL, 16, 128)
        ls[p][a, :, :, :128] = low.astype(BF16)
        high = dbuf[pl.ds(512, 256), :128].reshape(NL, 8, 128)
        tail = width - 128
        if tail > 0:
            at = lax.broadcasted_iota(jnp.int32, (512, 128), 1)
            first = jnp.where(at < tail, dbuf[pl.ds(0, 512), 128:], 0.0).reshape(NL, 16, 128)
            last = jnp.where(at[:256] < tail, dbuf[pl.ds(512, 256), 128:], 0.0)
            ends = first[:, :8] + (
                pltpu.roll(first[:, 8:].reshape(256, 128), tail, 1)
                + pltpu.roll(last, 2 * tail, 1)
            ).reshape(NL, 8, 128)
        else:
            ends = jnp.zeros((NL, 8, 128), F32)
        ls[p][a, :, :, 128:] = jnp.concatenate([high, ends], axis=1).astype(BF16)
        send_lat(a, p)

    def analyse_lat(a, p):
        count = PARTS[p][1]
        tail = WIDTH[p] - 128
        at = lanes(NL)
        wait_lat(a, p, lrs)
        dbuf[pl.ds(0, 512), :] = dot(perm[...], lr[p][a].reshape(512, 256))
        for kk in range(K):
            base, shift = divmod(SLOT * kk, 128)
            i, t = (kk, 0) if kk < 16 else (kk - 16, 1)
            main = dbuf[pl.ds(NL * i, NL), 128 * t : 128 * (t + 1)]
            main = pltpu.roll(main, shift, 1) if shift else main
            ring[kk, :, :128] = main
            if tail > 0:
                end = dbuf[pl.ds(NL * (8 + kk % 8), NL), 128:]
                turn = (shift - tail * (kk // 8)) % 128
                end = pltpu.roll(end, turn, 1) if turn else end
                ring[kk, :, 128:256] = jnp.where(at < shift, main, end) if shift else end
                ring[kk, :, 256:384] = end
            else:
                ring[kk, :, 128:256] = main
        for q in range(Q):
            start = count * q

            def pick(kk, t):
                t -= SLOT * kk // 128
                return ring[kk, :, 128 * t : 128 * (t + 1)]

            tiles = merge(NL, start, SLOT, K, pick)
            xform[pl.ds(NL * q, NL), :] = shift_left(tiles, start % 128)[:, : SLOT * K]
        strans[...] = jnp.transpose(xform[...]).astype(BF16)

    def synth_lat(p):
        count = PARTS[p][1]
        tail = WIDTH[p] - 128
        at = lanes(NL)
        xform[...] = jnp.transpose(sback[...])
        blank = jnp.zeros((NL, 128), F32)
        for q in range(Q):
            row = jnp.concatenate([xform[pl.ds(NL * q, NL), :], blank], axis=1)
            shift = count * q % 128
            ring[q] = pltpu.roll(row, shift, 1) if shift else row

        def column(kk):
            def pick(q, t):
                t -= count * q // 128
                return ring[q, :, 128 * t : 128 * (t + 1)]

            tiles = merge(NL, SLOT * kk, count, Q, pick)
            return shift_left(tiles, SLOT * kk % 128)

        for i in range(16):
            low = column(i)
            ring[Q + i % 8, :, 128 * (i // 8) : 128 * (i // 8 + 1)] = low[:, :128]
            if tail > 0:
                done = low[:, 128:256]
                if i < 8:
                    ring[Q + i, :, 256:384] = done
                else:
                    old = ring[Q + i - 8, :, 256:384]
                    ring[Q + i - 8, :, 256:384] = jnp.where(at >= tail, pltpu.roll(done, tail, 1), old)
        for i in range(8):
            high = column(16 + i)
            low = ring[Q + i, :, :128]
            xbuf[pl.ds(NL * i, NL), :] = jnp.concatenate([low, high[:, :128]], axis=1).astype(BF16)
            ends = blank
            if tail > 0:
                ends = jnp.where(
                    at >= 2 * tail, pltpu.roll(high[:, 128:256], 2 * tail, 1), ring[Q + i, :, 256:384]
                )
            low = ring[Q + i, :, 128:256]
            xbuf[pl.ds(NL * (8 + i), NL), :] = jnp.concatenate([low, ends], axis=1).astype(BF16)
        moved = dot(permt[...], xbuf[pl.ds(0, 512), :]).astype(BF16)
        ls[p][2] = moved.reshape(NL, 16, 256)
        send_lat(2, p)

    def synth_lon(p):
        width = WIDTH[p]
        tail = width - 128
        wait_lat(2, p, lrs)
        got = lr[p][2]
        xbuf[pl.ds(0, 512), :128] = got[:, :, :128].reshape(512, 128)
        second = got[:, :, 128:].astype(F32)
        xbuf[pl.ds(512, 256), :128] = second[:, :8].reshape(256, 128).astype(BF16)
        if tail > 0:
            ends = second[:, 8:].reshape(256, 128)
            one = pltpu.roll(ends, 128 - tail, 1)
            two = pltpu.roll(ends, 128 - 2 * tail, 1)
            both = jnp.concatenate([ends.reshape(NL, 8, 128), one.reshape(NL, 8, 128)], axis=1)
            xbuf[pl.ds(0, 512), 128:] = both.reshape(512, 128).astype(BF16)
            xbuf[pl.ds(512, 256), 128:] = two.astype(BF16)
        else:
            xbuf[:, 128:] = jnp.zeros((768, 128), BF16)
        at = lax.broadcasted_iota(jnp.int32, (256, 256), 1)
        tiles = [None] * TILES[p]
        for g in range(GROUPS):
            base, shift = divmod(width * g, 128)
            value = dot(bwd[pl.ds(256 * g, 256), :], xbuf[...])
            value = jnp.where(at < width, value, 0.0)
            value = pltpu.roll(value, shift, 1) if shift else value
            for t in range(2):
                if base + t < TILES[p]:
                    piece = value[:, 128 * t : 128 * (t + 1)]
                    old = tiles[base + t]
                    tiles[base + t] = piece if old is None else old + piece
        for t in range(TILES[p]):
            zs[p][2, :, :, 128 * t : 128 * (t + 1)] = tiles[t].astype(BF16).reshape(NZ, 16, 128)
        send_lon(2, p)

    def unpack(p):
        first, count = PARTS[p]
        wait_lon(2, p, zrs)
        for z in range(NZ):
            for g in range(GROUPS):
                base, shift = divmod(WIDTH[p] * g, 128)
                window = [zr[p][2, z, :, 128 * t : 128 * (t + 1)] for t in range(base, min(base + 2, TILES[p]))]
                window += [window[-1]] * (3 - len(window))
                turn = (C * z + first - shift) % RING
                wide = jnp.concatenate(window, axis=1)
                pbuf[z, 16 * g : 16 * (g + 1), :] = pltpu.roll(wide, turn, 1) if turn else wide
        at = lanes(N)
        for q in range(Q):
            start = first + count * q
            tiles = []
            for t in range(3):
                low = 128 * t - start
                z = low // C
                value = pbuf[z % NZ, :, 128 * t : 128 * (t + 1)]
                while C * (z + 1) - low < 128:
                    z += 1
                    value = jnp.where(
                        at >= C * z - low, pbuf[z % NZ, :, 128 * t : 128 * (t + 1)], value
                    )
                tiles.append(value)
            whole = shift_left(tiles, count * q)
            if p == 0:
                grad_out[q] = whole
            else:
                for t in range(3):
                    span = slice(128 * t, 128 * (t + 1))
                    inner = lax.rem(at + 128 * t, C)
                    grad_out[q, :, span] = jnp.where(inner < first, grad_out[q, :, span], whole[:, span])

    loads[0].wait()
    pack(0, 0)
    pack(0, 1)
    pl.semaphore_wait(barrier, len(greeted))
    for d in (4, 12):
        pl.semaphore_signal(far_sem, inc=1, device_id=ring_peer(d), device_id_type=MESH)
    for d in (2, 1, 3):
        pl.semaphore_signal(col_sem, inc=1, device_id=column_peer(d), device_id_type=MESH)
    send_lon(0, 0, near[::-1], False)
    pl.semaphore_wait(far_sem, 2)
    send_lon(0, 0, far)
    send_lon(0, 1)
    loads[1].wait()
    pack(1, 0)
    send_lon(1, 0)
    pack(1, 1)
    send_lon(1, 1)

    perm[...] = one_hot(512, lambda r: (r & (NL - 1)) * 16 + (r >> 5))
    permt[...] = one_hot(512, lambda r: (r & 15) * NL + (r >> 4))
    order = one_hot(LATS, lambda r: (r & (NL - 1)) * Q + (r >> 5))
    loads[2].wait()

    def reorder(m, carry):
        legp[m] = dot(order, leg[m]).astype(BF16)
        return carry

    lax.fori_loop(0, M, reorder, 0, unroll=2)
    loads[5].wait()
    gain[0] = filt[:, :SLOT]
    for r in range(2):
        first, count = PARTS[1]
        gain[1, r, :count] = filt[r, first:]
        gain[1, r, count:] = jnp.zeros((SLOT - count, DEGREES), F32)
    loads[3].wait()
    loads[4].wait()

    def spectrum(m):
        rows = pl.ds(pl.multiple_of(2 * SLOT * m, 2 * SLOT), 2 * SLOT)
        return dot(strans[rows, :], legp[m])

    def filter_cot(p):
        def analyse(m, carry):
            coef[p, m] = spectrum(m)
            return carry

        lax.fori_loop(0, M, analyse, 0, unroll=4)

        def synth(m, carry):
            re, im = coef[p, m, :SLOT], coef[p, m, SLOT:]
            back = jnp.concatenate(
                [gain[p, 0] * re + gain[p, 1] * im, gain[p, 0] * im - gain[p, 1] * re], axis=0
            ).astype(BF16)
            rows = pl.ds(pl.multiple_of(2 * SLOT * m, 2 * SLOT), 2 * SLOT)
            sback[rows, :] = lax.dot_general(
                back, legp[m], (((1,), (1,)), ((), ())), preferred_element_type=F32
            )
            return carry

        lax.fori_loop(0, M, synth, 0, unroll=4)

    def correlate(p):
        def one(m, carry):
            got = spectrum(m)
            in_re, in_im = got[:SLOT], got[SLOT:]
            cot_re, cot_im = coef[p, m, :SLOT], coef[p, m, SLOT:]
            acc[pl.ds(2 * SLOT * p, SLOT), :] += in_re * cot_re + in_im * cot_im
            acc[pl.ds(2 * SLOT * p + SLOT, SLOT), :] += in_re * cot_im - in_im * cot_re
            return carry

        lax.fori_loop(0, M, one, 0, unroll=4)

    acc[...] = jnp.zeros_like(acc)
    pl.semaphore_wait(col_sem, 3)
    analyse_lon(0, 0)
    analyse_lat(0, 0)
    analyse_lon(0, 1)
    filter_cot(0)
    synth_lat(0)
    analyse_lat(0, 1)
    filter_cot(1)
    synth_lat(1)
    synth_lon(0)
    analyse_lon(1, 0)
    synth_lon(1)
    analyse_lon(1, 1)
    analyse_lat(1, 0)
    correlate(0)
    analyse_lat(1, 1)
    correlate(1)
    gs[...] = jnp.transpose(acc[...])

    def send_sum(s, carry):
        to = lat ^ (NL - 1 - s)
        start = pl.multiple_of(Q * to - 4 * lax.rem(to, 2), 8)
        pltpu.make_async_remote_copy(
            src_ref=gs.at[pl.ds(start, 16)],
            dst_ref=gr.at[lat],
            send_sem=gss,
            recv_sem=grs,
            device_id=(to, lon),
            device_id_type=MESH,
        ).start()
        return carry

    lax.fori_loop(0, NL - 1, send_sum, 0)
    start = pl.multiple_of(Q * lat - 4 * lax.rem(lat, 2), 8)
    own = pltpu.make_async_copy(gs.at[pl.ds(start, 16)], gr.at[lat], own_sem.at[0])
    own.start()
    own.wait()
    some = gr.at[pl.ds(0, NL - 1)]
    unpack(0)
    pltpu.make_async_copy(some, some, grs).wait()
    total = jnp.sum(gr[...], axis=0)
    total = jnp.where(lax.rem(lat, 2) == 1, total[4:16], total[:12])
    for r in range(2):
        for p in range(2):
            first, count = PARTS[p]
            low = 2 * SLOT * p + SLOT * r
            filt_out[:, r, first : first + count] = total[:, low : low + count]
    unpack(1)

    for phase in range(3):
        for p in range(2):
            wait_lon(phase, p, zss)
            wait_lat(phase, p, lss)
    pltpu.make_async_copy(some, some, gss).wait()


def hand_over(grad_in, filt_in, grad_out, filt_out):
    grad_out[...] = grad_in[...]
    filt_out[...] = filt_in[...]


def local(grid_in, grid_cot, legendre, filters):
    fwd, bwd = fourier_tables()
    vmem = pltpu.VMEM
    any_space = pl.BlockSpec(memory_space=pl.ANY)
    outs = pl.pallas_call(
        kernel,
        out_shape=(
            jax.ShapeDtypeStruct((Q, N, CHANNELS), BF16),
            jax.ShapeDtypeStruct((Q, 2, C), F32),
        ),
        in_specs=[any_space] * 6,
        out_specs=(pl.BlockSpec(memory_space=vmem), pl.BlockSpec(memory_space=vmem)),
        scratch_shapes=[
            vmem((2, Q, N, CHANNELS), BF16),
            vmem((M, LATS, DEGREES), BF16),
            vmem((M, LATS, DEGREES), BF16),
            vmem((2, C, DEGREES), F32),
            vmem((2 * DEGREES, LONS), BF16),
            vmem((LONS, 2 * DEGREES), BF16),
            vmem((512, 512), BF16),
            vmem((512, 512), BF16),
            vmem((K, NL, 512), F32),
            vmem((NZ, N, RING), BF16),
            vmem((2, 2, SLOT, DEGREES), F32),
            vmem((768, 256), BF16),
            vmem((768, 256), F32),
            vmem((LATS, SLOT * K), F32),
            vmem((SLOT * K, LATS), BF16),
            vmem((SLOT * K, LATS), F32),
            vmem((2, M, 2 * SLOT, DEGREES), F32),
            vmem((128, DEGREES), F32),
            vmem((3, NZ, 16, 128 * TILES[0]), BF16),
            vmem((3, NZ, 16, 128 * TILES[1]), BF16),
            vmem((3, NZ, 16, 128 * TILES[0]), BF16),
            vmem((3, NZ, 16, 128 * TILES[1]), BF16),
            vmem((3, NL, 16, 256), BF16),
            vmem((3, NL, 16, 256), BF16),
            vmem((3, NL, 16, 256), BF16),
            vmem((3, NL, 16, 256), BF16),
            vmem((DEGREES, 128), F32),
            vmem((NL, 16, 128), F32),
            pltpu.SemaphoreType.DMA((6,)),
            pltpu.SemaphoreType.DMA((1,)),
            pltpu.SemaphoreType.DMA((3, 2)),
            pltpu.SemaphoreType.DMA((3, 2)),
            pltpu.SemaphoreType.DMA((3, 2)),
            pltpu.SemaphoreType.DMA((3, 2)),
            pltpu.SemaphoreType.DMA,
            pltpu.SemaphoreType.DMA,
            pltpu.SemaphoreType.REGULAR,
            pltpu.SemaphoreType.REGULAR,
        ],
        compiler_params=pltpu.CompilerParams(
            collective_id=0, has_side_effects=True, vmem_limit_bytes=56 * 1024 * 1024
        ),
    )(
        grid_in, grid_cot, legendre, jnp.transpose(filters, (1, 2, 0)), jnp.asarray(fwd), jnp.asarray(bwd)
    )
    return pl.pallas_call(
        hand_over,
        out_shape=tuple(jax.ShapeDtypeStruct(out.shape, out.dtype) for out in outs),
        in_specs=[pl.BlockSpec(memory_space=vmem)] * 2,
        out_specs=(pl.BlockSpec(memory_space=vmem), pl.BlockSpec(memory_space=vmem)),
    )(*outs)


def solution(mesh):
    return jax.shard_map(
        local,
        mesh=mesh,
        in_specs=(
            P("lat", "lon", None),
            P("lat", "lon", None),
            P("lat", None, None),
            P(None, None, "lon"),
        ),
        out_specs=(P("lat", "lon", None), P("lat", None, "lon")),
        check_vma=False,
    )
```

```python
import math

import jax
import jax.numpy as jnp
import ml_dtypes
import numpy as np
from jax import lax
from jax.experimental import pallas as pl
from jax.experimental.pallas import tpu as pltpu
from jax.sharding import PartitionSpec as P

MESH = pl.DeviceIdType.MESH
BF16 = jnp.bfloat16
F32 = jnp.float32

NZ, NL = 16, 32
LATS, LONS, DEGREES, CHANNELS = 384, 768, 384, 384
Q, N, C = LATS // NL, LONS // NZ, CHANNELS // NZ
M = DEGREES // NL
K = 2 * M
RING = 384
GROUPS = N // 16
SLOT = 16

PARTS = ((0, 14), (14, 10))
WIDTH = tuple(Q * count for _, count in PARTS)
TILES = tuple(-(-GROUPS * w // 128) for w in WIDTH)


def fourier_tables():
    points = np.arange(LONS, dtype=np.int64)[:, None]
    order = np.arange(DEGREES, dtype=np.int64)[None, :]
    phases = (points * order) % LONS
    angles = phases.astype(np.float32) * np.float32(2.0 * math.pi / LONS)
    pair = np.stack([np.cos(angles), -np.sin(angles)], axis=2) * np.float32(LONS ** (-0.5))
    table = pair.reshape(LONS, 2 * DEGREES).astype(ml_dtypes.bfloat16)
    n_of = np.arange(LONS).reshape(NZ, GROUPS, 16).transpose(1, 0, 2).reshape(-1)
    k = np.arange(2 * DEGREES).reshape(NL, 2 * M)
    k_of = np.concatenate([k[:, :16].reshape(-1), k[:, 16:].reshape(-1)])
    back = table[n_of][:, k_of]
    return np.ascontiguousarray(back.T), np.ascontiguousarray(back)


def lanes(rows):
    return lax.broadcasted_iota(jnp.int32, (rows, 128), 1)


def merge(rows, start, step, count, pick):
    at = lanes(rows)
    tiles = []
    for t in range(start // 128, (start + step * count - 1) // 128 + 1):
        value = None
        for i in range(count):
            low, high = start + step * i - 128 * t, start + step * (i + 1) - 128 * t
            if high <= 0 or low >= 128:
                continue
            block = pick(i, t)
            value = block if value is None else jnp.where(at >= low, block, value)
        tiles.append(value)
    return tiles


def shift_left(tiles, shift):
    wide = jnp.concatenate(tiles, axis=1) if len(tiles) > 1 else tiles[0]
    size = 128 * len(tiles)
    return pltpu.roll(wide, (size - shift) % size, 1) if shift % size else wide


def one_hot(size, column_of):
    row = lax.broadcasted_iota(jnp.int32, (size, size), 0)
    column = lax.broadcasted_iota(jnp.int32, (size, size), 1)
    return jnp.where(column == column_of(row), 1.0, 0.0).astype(BF16)


def dot(a, b):
    return jnp.dot(a, b, preferred_element_type=F32)


def kernel(
    in_hbm, cot_hbm, leg_hbm, filt_hbm, fwd_hbm, bwd_hbm,
    grad_out, filt_out,
    grid, leg, legp, filt, fwd, bwd, perm, permt, ring, pbuf, gain, xbuf, dbuf, xform, strans, sback, coef, acc,
    zs_a, zs_b, zr_a, zr_b, ls_a, ls_b, lr_a, lr_b, gs, gr,
    load_sem, own_sem, zss, zrs, lss, lrs, gss, grs, far_sem, col_sem,
):
    lat, lon = lax.axis_index("lat"), lax.axis_index("lon")
    zs, zr, ls, lr = (zs_a, zs_b), (zr_a, zr_b), (ls_a, ls_b), (lr_a, lr_b)

    def ring_peer(d):
        return (lat, lax.rem(lon + d, NZ))

    def row_peer(d):
        return ((lat & 6) | ((lat ^ d) & 25), lon)

    def column_peer(d):
        return ((lat & 25) | ((lat + 2 * d) & 6), lon)

    barrier = pltpu.get_barrier_semaphore()
    near = (4, 12, 3, 13, 2, 14, 1, 15)
    far = (8, 7, 9, 6, 10, 5, 11)
    greeted = [ring_peer(d) for d in near]
    greeted += [row_peer(d) for d in (25, 24, 17, 16, 9, 8, 1)]
    greeted += [column_peer(d) for d in (2, 1, 3)]
    for peer in greeted:
        pl.semaphore_signal(barrier, inc=1, device_id=peer, device_id_type=MESH)
    loads = [
        pltpu.make_async_copy(cot_hbm, grid.at[0], load_sem.at[0]),
        pltpu.make_async_copy(in_hbm, grid.at[1], load_sem.at[1]),
        pltpu.make_async_copy(leg_hbm, leg, load_sem.at[2]),
        pltpu.make_async_copy(fwd_hbm, fwd, load_sem.at[3]),
        pltpu.make_async_copy(bwd_hbm, bwd, load_sem.at[4]),
        pltpu.make_async_copy(filt_hbm, filt, load_sem.at[5]),
    ]
    for load in loads:
        load.start()
    def send_lon(phase, p, distances=far + near, own=True):
        for d in distances:
            to = lax.rem(lon + d, NZ)
            pltpu.make_async_remote_copy(
                src_ref=zs[p].at[phase, to],
                dst_ref=zr[p].at[phase, lon],
                send_sem=zss.at[phase, p],
                recv_sem=zrs.at[phase, p],
                device_id=(lat, to),
                device_id_type=MESH,
            ).start()
        if own:
            zr[p][phase, lon] = zs[p][phase, lon]

    def wait_lon(phase, p, sem):
        some = zr[p].at[phase, pl.ds(0, NZ - 1)]
        pltpu.make_async_copy(some, some, sem.at[phase, p]).wait()

    def send_lat(phase, p):
        def step(s, carry):
            to = lat ^ (NL - 1 - s)
            pltpu.make_async_remote_copy(
                src_ref=ls[p].at[phase, to],
                dst_ref=lr[p].at[phase, lat],
                send_sem=lss.at[phase, p],
                recv_sem=lrs.at[phase, p],
                device_id=(to, lon),
                device_id_type=MESH,
            ).start()
            return carry

        lax.fori_loop(0, NL - 1, step, 0)
        lr[p][phase, lat] = ls[p][phase, lat]

    def wait_lat(phase, p, sem):
        some = lr[p].at[phase, pl.ds(0, NL - 1)]
        pltpu.make_async_copy(some, some, sem.at[phase, p]).wait()

    def pack(a, p):
        first, count = PARTS[p]
        at = lanes(16)
        for q in range(Q):
            wide = grid[a, q]
            pbuf[q] = pltpu.roll(wide, count * q, 1) if q else wide
        for z in range(NZ):
            start = C * z + first
            moved = jnp.concatenate(
                merge(N, start, count, Q, lambda q, t: pbuf[q, :, 128 * (t % 3) : 128 * (t % 3) + 128]),
                axis=1,
            )
            size = moved.shape[1]
            if size == 128:
                moved = jnp.concatenate([moved, moved], axis=1)
                size = 256
            tiles = [None] * (TILES[p] + 1)
            for g in range(GROUPS):
                base, shift = divmod(WIDTH[p] * g, 128)
                turn = (shift - start % 128) % size
                rows = moved[16 * g : 16 * (g + 1)]
                rows = pltpu.roll(rows, turn, 1) if turn else rows
                old = tiles[base]
                tiles[base] = rows[:, :128] if old is None else jnp.where(at >= shift, rows[:, :128], old)
                tiles[base + 1] = rows[:, 128:256]
            zs[p][a, z] = jnp.concatenate(tiles[: TILES[p]], axis=1)

    def analyse_lon(a, p):
        width = WIDTH[p]
        wait_lon(a, p, zrs)
        for g in range(GROUPS):
            base, shift = divmod(width * g, 128)
            window = zr[p][a, :, :, 128 * base : 128 * base + 256].reshape(256, 256)
            if shift:
                window = pltpu.roll(window.astype(F32), 256 - shift, 1).astype(BF16)
            xbuf[pl.ds(256 * g, 256), :] = window
        for r in range(3):
            dbuf[pl.ds(256 * r, 256), :] = dot(fwd[pl.ds(256 * r, 256), :], xbuf[...])
        low = dbuf[pl.ds(0, 512), :128].reshape(NL, 16, 128)
        ls[p][a, :, :, :128] = low.astype(BF16)
        high = dbuf[pl.ds(512, 256), :128].reshape(NL, 8, 128)
        tail = width - 128
        if tail > 0:
            at = lax.broadcasted_iota(jnp.int32, (512, 128), 1)
            first = jnp.where(at < tail, dbuf[pl.ds(0, 512), 128:], 0.0).reshape(NL, 16, 128)
            last = jnp.where(at[:256] < tail, dbuf[pl.ds(512, 256), 128:], 0.0)
            ends = first[:, :8] + (
                pltpu.roll(first[:, 8:].reshape(256, 128), tail, 1)
                + pltpu.roll(last, 2 * tail, 1)
            ).reshape(NL, 8, 128)
        else:
            ends = jnp.zeros((NL, 8, 128), F32)
        ls[p][a, :, :, 128:] = jnp.concatenate([high, ends], axis=1).astype(BF16)
        send_lat(a, p)

    def analyse_lat(a, p):
        count = PARTS[p][1]
        tail = WIDTH[p] - 128
        at = lanes(NL)
        wait_lat(a, p, lrs)
        dbuf[pl.ds(0, 512), :] = dot(perm[...], lr[p][a].reshape(512, 256))
        for kk in range(K):
            base, shift = divmod(SLOT * kk, 128)
            i, t = (kk, 0) if kk < 16 else (kk - 16, 1)
            main = dbuf[pl.ds(NL * i, NL), 128 * t : 128 * (t + 1)]
            main = pltpu.roll(main, shift, 1) if shift else main
            ring[kk, :, :128] = main
            if tail > 0:
                end = dbuf[pl.ds(NL * (8 + kk % 8), NL), 128:]
                turn = (shift - tail * (kk // 8)) % 128
                end = pltpu.roll(end, turn, 1) if turn else end
                ring[kk, :, 128:256] = jnp.where(at < shift, main, end) if shift else end
                ring[kk, :, 256:384] = end
            else:
                ring[kk, :, 128:256] = main
        for q in range(Q):
            start = count * q

            def pick(kk, t):
                t -= SLOT * kk // 128
                return ring[kk, :, 128 * t : 128 * (t + 1)]

            tiles = merge(NL, start, SLOT, K, pick)
            xform[pl.ds(NL * q, NL), :] = shift_left(tiles, start % 128)[:, : SLOT * K]
        strans[...] = jnp.transpose(xform[...]).astype(BF16)

    def synth_lat(p):
        count = PARTS[p][1]
        tail = WIDTH[p] - 128
        at = lanes(NL)
        xform[...] = jnp.transpose(sback[...])
        blank = jnp.zeros((NL, 128), F32)
        for q in range(Q):
            row = jnp.concatenate([xform[pl.ds(NL * q, NL), :], blank], axis=1)
            shift = count * q % 128
            ring[q] = pltpu.roll(row, shift, 1) if shift else row

        def column(kk):
            def pick(q, t):
                t -= count * q // 128
                return ring[q, :, 128 * t : 128 * (t + 1)]

            tiles = merge(NL, SLOT * kk, count, Q, pick)
            return shift_left(tiles, SLOT * kk % 128)

        for i in range(16):
            low = column(i)
            ring[Q + i % 8, :, 128 * (i // 8) : 128 * (i // 8 + 1)] = low[:, :128]
            if tail > 0:
                done = low[:, 128:256]
                if i < 8:
                    ring[Q + i, :, 256:384] = done
                else:
                    old = ring[Q + i - 8, :, 256:384]
                    ring[Q + i - 8, :, 256:384] = jnp.where(at >= tail, pltpu.roll(done, tail, 1), old)
        for i in range(8):
            high = column(16 + i)
            low = ring[Q + i, :, :128]
            xbuf[pl.ds(NL * i, NL), :] = jnp.concatenate([low, high[:, :128]], axis=1).astype(BF16)
            ends = blank
            if tail > 0:
                ends = jnp.where(
                    at >= 2 * tail, pltpu.roll(high[:, 128:256], 2 * tail, 1), ring[Q + i, :, 256:384]
                )
            low = ring[Q + i, :, 128:256]
            xbuf[pl.ds(NL * (8 + i), NL), :] = jnp.concatenate([low, ends], axis=1).astype(BF16)
        moved = dot(permt[...], xbuf[pl.ds(0, 512), :]).astype(BF16)
        ls[p][2] = moved.reshape(NL, 16, 256)
        send_lat(2, p)

    def synth_lon(p):
        width = WIDTH[p]
        tail = width - 128
        wait_lat(2, p, lrs)
        got = lr[p][2]
        xbuf[pl.ds(0, 512), :128] = got[:, :, :128].reshape(512, 128)
        second = got[:, :, 128:].astype(F32)
        xbuf[pl.ds(512, 256), :128] = second[:, :8].reshape(256, 128).astype(BF16)
        if tail > 0:
            ends = second[:, 8:].reshape(256, 128)
            one = pltpu.roll(ends, 128 - tail, 1)
            two = pltpu.roll(ends, 128 - 2 * tail, 1)
            both = jnp.concatenate([ends.reshape(NL, 8, 128), one.reshape(NL, 8, 128)], axis=1)
            xbuf[pl.ds(0, 512), 128:] = both.reshape(512, 128).astype(BF16)
            xbuf[pl.ds(512, 256), 128:] = two.astype(BF16)
        else:
            xbuf[:, 128:] = jnp.zeros((768, 128), BF16)
        at = lax.broadcasted_iota(jnp.int32, (256, 256), 1)
        tiles = [None] * TILES[p]
        for g in range(GROUPS):
            base, shift = divmod(width * g, 128)
            value = dot(bwd[pl.ds(256 * g, 256), :], xbuf[...])
            value = jnp.where(at < width, value, 0.0)
            value = pltpu.roll(value, shift, 1) if shift else value
            for t in range(2):
                if base + t < TILES[p]:
                    piece = value[:, 128 * t : 128 * (t + 1)]
                    old = tiles[base + t]
                    tiles[base + t] = piece if old is None else old + piece
        for t in range(TILES[p]):
            zs[p][2, :, :, 128 * t : 128 * (t + 1)] = tiles[t].astype(BF16).reshape(NZ, 16, 128)
        send_lon(2, p)

    def unpack(p):
        first, count = PARTS[p]
        wait_lon(2, p, zrs)
        for z in range(NZ):
            for g in range(GROUPS):
                base, shift = divmod(WIDTH[p] * g, 128)
                window = [zr[p][2, z, :, 128 * t : 128 * (t + 1)] for t in range(base, min(base + 2, TILES[p]))]
                window += [window[-1]] * (3 - len(window))
                turn = (C * z + first - shift) % RING
                wide = jnp.concatenate(window, axis=1)
                pbuf[z, 16 * g : 16 * (g + 1), :] = pltpu.roll(wide, turn, 1) if turn else wide
        at = lanes(N)
        for q in range(Q):
            start = first + count * q
            tiles = []
            for t in range(3):
                low = 128 * t - start
                z = low // C
                value = pbuf[z % NZ, :, 128 * t : 128 * (t + 1)]
                while C * (z + 1) - low < 128:
                    z += 1
                    value = jnp.where(
                        at >= C * z - low, pbuf[z % NZ, :, 128 * t : 128 * (t + 1)], value
                    )
                tiles.append(value)
            whole = shift_left(tiles, count * q)
            if p == 0:
                grad_out[q] = whole
            else:
                for t in range(3):
                    span = slice(128 * t, 128 * (t + 1))
                    inner = lax.rem(at + 128 * t, C)
                    grad_out[q, :, span] = jnp.where(inner < first, grad_out[q, :, span], whole[:, span])

    loads[0].wait()
    pack(0, 0)
    pack(0, 1)
    pl.semaphore_wait(barrier, len(greeted))
    for d in (4, 12):
        pl.semaphore_signal(far_sem, inc=1, device_id=ring_peer(d), device_id_type=MESH)
    for d in (2, 1, 3):
        pl.semaphore_signal(col_sem, inc=1, device_id=column_peer(d), device_id_type=MESH)
    send_lon(0, 0, near[::-1], False)
    pl.semaphore_wait(far_sem, 2)
    send_lon(0, 0, far)
    send_lon(0, 1)
    loads[1].wait()
    pack(1, 0)
    send_lon(1, 0)
    pack(1, 1)
    send_lon(1, 1)

    perm[...] = one_hot(512, lambda r: (r & (NL - 1)) * 16 + (r >> 5))
    permt[...] = one_hot(512, lambda r: (r & 15) * NL + (r >> 4))
    order = one_hot(LATS, lambda r: (r & (NL - 1)) * Q + (r >> 5))
    loads[2].wait()

    def reorder(m, carry):
        legp[m] = dot(order, leg[m]).astype(BF16)
        return carry

    lax.fori_loop(0, M, reorder, 0, unroll=2)
    loads[5].wait()
    gain[0] = filt[:, :SLOT]
    for r in range(2):
        first, count = PARTS[1]
        gain[1, r, :count] = filt[r, first:]
        gain[1, r, count:] = jnp.zeros((SLOT - count, DEGREES), F32)
    loads[3].wait()
    loads[4].wait()

    def spectrum(m):
        rows = pl.ds(pl.multiple_of(2 * SLOT * m, 2 * SLOT), 2 * SLOT)
        return dot(strans[rows, :], legp[m])

    def filter_cot(p):
        def analyse(m, carry):
            coef[p, m] = spectrum(m)
            return carry

        lax.fori_loop(0, M, analyse, 0, unroll=4)

        def synth(m, carry):
            re, im = coef[p, m, :SLOT], coef[p, m, SLOT:]
            back = jnp.concatenate(
                [gain[p, 0] * re + gain[p, 1] * im, gain[p, 0] * im - gain[p, 1] * re], axis=0
            ).astype(BF16)
            rows = pl.ds(pl.multiple_of(2 * SLOT * m, 2 * SLOT), 2 * SLOT)
            sback[rows, :] = lax.dot_general(
                back, legp[m], (((1,), (1,)), ((), ())), preferred_element_type=F32
            )
            return carry

        lax.fori_loop(0, M, synth, 0, unroll=4)

    def correlate(p):
        def one(m, carry):
            got = spectrum(m)
            in_re, in_im = got[:SLOT], got[SLOT:]
            cot_re, cot_im = coef[p, m, :SLOT], coef[p, m, SLOT:]
            acc[pl.ds(2 * SLOT * p, SLOT), :] += in_re * cot_re + in_im * cot_im
            acc[pl.ds(2 * SLOT * p + SLOT, SLOT), :] += in_re * cot_im - in_im * cot_re
            return carry

        lax.fori_loop(0, M, one, 0, unroll=4)

    acc[...] = jnp.zeros_like(acc)
    pl.semaphore_wait(col_sem, 3)
    analyse_lon(0, 0)
    analyse_lat(0, 0)
    analyse_lon(0, 1)
    filter_cot(0)
    synth_lat(0)
    analyse_lat(0, 1)
    filter_cot(1)
    synth_lat(1)
    synth_lon(0)
    analyse_lon(1, 0)
    synth_lon(1)
    analyse_lon(1, 1)
    analyse_lat(1, 0)
    correlate(0)
    analyse_lat(1, 1)
    correlate(1)
    gs[...] = jnp.transpose(acc[...])

    def send_sum(s, carry):
        to = lat ^ (NL - 1 - s)
        start = pl.multiple_of(Q * to - 4 * lax.rem(to, 2), 8)
        pltpu.make_async_remote_copy(
            src_ref=gs.at[pl.ds(start, 16)],
            dst_ref=gr.at[lat],
            send_sem=gss,
            recv_sem=grs,
            device_id=(to, lon),
            device_id_type=MESH,
        ).start()
        return carry

    lax.fori_loop(0, NL - 1, send_sum, 0)
    start = pl.multiple_of(Q * lat - 4 * lax.rem(lat, 2), 8)
    own = pltpu.make_async_copy(gs.at[pl.ds(start, 16)], gr.at[lat], own_sem.at[0])
    own.start()
    own.wait()
    some = gr.at[pl.ds(0, NL - 1)]
    unpack(0)
    pltpu.make_async_copy(some, some, grs).wait()
    total = jnp.sum(gr[...], axis=0)
    total = jnp.where(lax.rem(lat, 2) == 1, total[4:16], total[:12])
    for r in range(2):
        for p in range(2):
            first, count = PARTS[p]
            low = 2 * SLOT * p + SLOT * r
            filt_out[:, r, first : first + count] = total[:, low : low + count]
    for phase in range(3):
        for p in range(2):
            if (phase, p) != (2, 1):
                wait_lon(phase, p, zss)
            wait_lat(phase, p, lss)
    pltpu.make_async_copy(some, some, gss).wait()
    unpack(1)
    wait_lon(2, 1, zss)


def local(grid_in, grid_cot, legendre, filters):
    fwd, bwd = fourier_tables()
    vmem = pltpu.VMEM
    any_space = pl.BlockSpec(memory_space=pl.ANY)
    outs = pl.pallas_call(
        kernel,
        out_shape=(vmem((Q, N, CHANNELS), BF16), vmem((Q, 2, C), F32)),
        in_specs=[any_space] * 6,
        out_specs=(pl.BlockSpec(memory_space=vmem), pl.BlockSpec(memory_space=vmem)),
        scratch_shapes=[
            vmem((2, Q, N, CHANNELS), BF16),
            vmem((M, LATS, DEGREES), BF16),
            vmem((M, LATS, DEGREES), BF16),
            vmem((2, C, DEGREES), F32),
            vmem((2 * DEGREES, LONS), BF16),
            vmem((LONS, 2 * DEGREES), BF16),
            vmem((512, 512), BF16),
            vmem((512, 512), BF16),
            vmem((K, NL, 512), F32),
            vmem((NZ, N, RING), BF16),
            vmem((2, 2, SLOT, DEGREES), F32),
            vmem((768, 256), BF16),
            vmem((768, 256), F32),
            vmem((LATS, SLOT * K), F32),
            vmem((SLOT * K, LATS), BF16),
            vmem((SLOT * K, LATS), F32),
            vmem((2, M, 2 * SLOT, DEGREES), F32),
            vmem((128, DEGREES), F32),
            vmem((3, NZ, 16, 128 * TILES[0]), BF16),
            vmem((3, NZ, 16, 128 * TILES[1]), BF16),
            vmem((3, NZ, 16, 128 * TILES[0]), BF16),
            vmem((3, NZ, 16, 128 * TILES[1]), BF16),
            vmem((3, NL, 16, 256), BF16),
            vmem((3, NL, 16, 256), BF16),
            vmem((3, NL, 16, 256), BF16),
            vmem((3, NL, 16, 256), BF16),
            vmem((DEGREES, 128), F32),
            vmem((NL, 16, 128), F32),
            pltpu.SemaphoreType.DMA((6,)),
            pltpu.SemaphoreType.DMA((1,)),
            pltpu.SemaphoreType.DMA((3, 2)),
            pltpu.SemaphoreType.DMA((3, 2)),
            pltpu.SemaphoreType.DMA((3, 2)),
            pltpu.SemaphoreType.DMA((3, 2)),
            pltpu.SemaphoreType.DMA,
            pltpu.SemaphoreType.DMA,
            pltpu.SemaphoreType.REGULAR,
            pltpu.SemaphoreType.REGULAR,
        ],
        compiler_params=pltpu.CompilerParams(
            collective_id=0, has_side_effects=True, vmem_limit_bytes=56 * 1024 * 1024
        ),
    )(
        grid_in, grid_cot, legendre, jnp.transpose(filters, (1, 2, 0)), jnp.asarray(fwd), jnp.asarray(bwd)
    )
    return outs


def solution(mesh):
    return jax.shard_map(
        local,
        mesh=mesh,
        in_specs=(
            P("lat", "lon", None),
            P("lat", "lon", None),
            P("lat", None, None),
            P(None, None, "lon"),
        ),
        out_specs=(P("lat", "lon", None), P("lat", None, "lon")),
        check_vma=False,
    )
```

```python
import math

import jax
import jax.numpy as jnp
import ml_dtypes
import numpy as np
from jax import lax
from jax.experimental import pallas as pl
from jax.experimental.pallas import tpu as pltpu
from jax.sharding import PartitionSpec as P

MESH = pl.DeviceIdType.MESH
BF16 = jnp.bfloat16
F32 = jnp.float32

NZ, NL = 16, 32
LATS, LONS, DEGREES, CHANNELS = 384, 768, 384, 384
Q, N, C = LATS // NL, LONS // NZ, CHANNELS // NZ
M = DEGREES // NL
K = 2 * M
RING = 384
GROUPS = N // 16
SLOT = 16

PARTS = ((0, 14), (14, 10))
WIDTH = tuple(Q * count for _, count in PARTS)
TILES = tuple(-(-GROUPS * w // 128) for w in WIDTH)


def fourier_tables():
    points = np.arange(LONS, dtype=np.int64)[:, None]
    order = np.arange(DEGREES, dtype=np.int64)[None, :]
    phases = (points * order) % LONS
    angles = phases.astype(np.float32) * np.float32(2.0 * math.pi / LONS)
    pair = np.stack([np.cos(angles), -np.sin(angles)], axis=2) * np.float32(LONS ** (-0.5))
    table = pair.reshape(LONS, 2 * DEGREES).astype(ml_dtypes.bfloat16)
    n_of = np.arange(LONS).reshape(NZ, GROUPS, 16).transpose(1, 0, 2).reshape(-1)
    k = np.arange(2 * DEGREES).reshape(NL, 2 * M)
    k_of = np.concatenate([k[:, :16].reshape(-1), k[:, 16:].reshape(-1)])
    back = table[n_of][:, k_of]
    return np.ascontiguousarray(back.T), np.ascontiguousarray(back)


def lanes(rows):
    return lax.broadcasted_iota(jnp.int32, (rows, 128), 1)


def merge(rows, start, step, count, pick):
    at = lanes(rows)
    tiles = []
    for t in range(start // 128, (start + step * count - 1) // 128 + 1):
        value = None
        for i in range(count):
            low, high = start + step * i - 128 * t, start + step * (i + 1) - 128 * t
            if high <= 0 or low >= 128:
                continue
            block = pick(i, t)
            value = block if value is None else jnp.where(at >= low, block, value)
        tiles.append(value)
    return tiles


def shift_left(tiles, shift):
    wide = jnp.concatenate(tiles, axis=1) if len(tiles) > 1 else tiles[0]
    size = 128 * len(tiles)
    return pltpu.roll(wide, (size - shift) % size, 1) if shift % size else wide


def one_hot(size, column_of):
    row = lax.broadcasted_iota(jnp.int32, (size, size), 0)
    column = lax.broadcasted_iota(jnp.int32, (size, size), 1)
    return jnp.where(column == column_of(row), 1.0, 0.0).astype(BF16)


def dot(a, b):
    return jnp.dot(a, b, preferred_element_type=F32)


def kernel(
    in_hbm, cot_hbm, leg_hbm, filt_hbm, fwd_hbm, bwd_hbm,
    grad_out, filt_out,
    grid, leg, legp, filt, fwd, bwd, perm, permt, ring, pbuf, gain, xbuf, dbuf, xform, strans, sback, coef, acc,
    zs_a, zs_b, zr_a, zr_b, ls_a, ls_b, lr_a, lr_b, gs, gr,
    load_sem, own_sem, zss, zrs, lss, lrs, gss, grs, far_sem, col_sem,
):
    lat, lon = lax.axis_index("lat"), lax.axis_index("lon")
    zs, zr, ls, lr = (zs_a, zs_b), (zr_a, zr_b), (ls_a, ls_b), (lr_a, lr_b)

    def ring_peer(d):
        return (lat, lax.rem(lon + d, NZ))

    def row_peer(d):
        return ((lat & 6) | ((lat ^ d) & 25), lon)

    def column_peer(d):
        return ((lat & 25) | ((lat + 2 * d) & 6), lon)

    barrier = pltpu.get_barrier_semaphore()
    near = (4, 12, 3, 13, 2, 14, 1, 15)
    far = (8, 7, 9, 6, 10, 5, 11)
    greeted = [ring_peer(d) for d in near]
    greeted += [row_peer(d) for d in (25, 24, 17, 16, 9, 8, 1)]
    greeted += [column_peer(d) for d in (2, 1, 3)]
    for peer in greeted:
        pl.semaphore_signal(barrier, inc=1, device_id=peer, device_id_type=MESH)
    loads = [
        pltpu.make_async_copy(cot_hbm, grid.at[0], load_sem.at[0]),
        pltpu.make_async_copy(in_hbm, grid.at[1], load_sem.at[1]),
        pltpu.make_async_copy(leg_hbm, leg, load_sem.at[2]),
        pltpu.make_async_copy(fwd_hbm, fwd, load_sem.at[3]),
        pltpu.make_async_copy(bwd_hbm, bwd, load_sem.at[4]),
        pltpu.make_async_copy(filt_hbm, filt, load_sem.at[5]),
    ]
    for load in loads:
        load.start()
    def send_lon(phase, p, distances=far + near, own=True):
        for d in distances:
            to = lax.rem(lon + d, NZ)
            pltpu.make_async_remote_copy(
                src_ref=zs[p].at[phase, to],
                dst_ref=zr[p].at[phase, lon],
                send_sem=zss.at[phase, p],
                recv_sem=zrs.at[phase, p],
                device_id=(lat, to),
                device_id_type=MESH,
            ).start()
        if own:
            zr[p][phase, lon] = zs[p][phase, lon]

    def wait_lon(phase, p, sem):
        some = zr[p].at[phase, pl.ds(0, NZ - 1)]
        pltpu.make_async_copy(some, some, sem.at[phase, p]).wait()

    def send_lat(phase, p):
        def step(s, carry):
            to = lat ^ (NL - 1 - s)
            pltpu.make_async_remote_copy(
                src_ref=ls[p].at[phase, to],
                dst_ref=lr[p].at[phase, lat],
                send_sem=lss.at[phase, p],
                recv_sem=lrs.at[phase, p],
                device_id=(to, lon),
                device_id_type=MESH,
            ).start()
            return carry

        lax.fori_loop(0, NL - 1, step, 0)
        lr[p][phase, lat] = ls[p][phase, lat]

    def wait_lat(phase, p, sem):
        some = lr[p].at[phase, pl.ds(0, NL - 1)]
        pltpu.make_async_copy(some, some, sem.at[phase, p]).wait()

    def pack(a, p):
        first, count = PARTS[p]
        at = lanes(16)
        for q in range(Q):
            wide = grid[a, q]
            pbuf[q] = pltpu.roll(wide, count * q, 1) if q else wide
        for z in range(NZ):
            start = C * z + first
            moved = jnp.concatenate(
                merge(N, start, count, Q, lambda q, t: pbuf[q, :, 128 * (t % 3) : 128 * (t % 3) + 128]),
                axis=1,
            )
            size = moved.shape[1]
            if size == 128:
                moved = jnp.concatenate([moved, moved], axis=1)
                size = 256
            tiles = [None] * (TILES[p] + 1)
            for g in range(GROUPS):
                base, shift = divmod(WIDTH[p] * g, 128)
                turn = (shift - start % 128) % size
                rows = moved[16 * g : 16 * (g + 1)]
                rows = pltpu.roll(rows, turn, 1) if turn else rows
                old = tiles[base]
                tiles[base] = rows[:, :128] if old is None else jnp.where(at >= shift, rows[:, :128], old)
                tiles[base + 1] = rows[:, 128:256]
            zs[p][a, z] = jnp.concatenate(tiles[: TILES[p]], axis=1)

    def analyse_lon(a, p):
        width = WIDTH[p]
        wait_lon(a, p, zrs)
        for g in range(GROUPS):
            base, shift = divmod(width * g, 128)
            window = zr[p][a, :, :, 128 * base : 128 * base + 256].reshape(256, 256)
            if shift:
                window = pltpu.roll(window.astype(F32), 256 - shift, 1).astype(BF16)
            xbuf[pl.ds(256 * g, 256), :] = window
        for r in range(3):
            dbuf[pl.ds(256 * r, 256), :] = dot(fwd[pl.ds(256 * r, 256), :], xbuf[...])
        low = dbuf[pl.ds(0, 512), :128].reshape(NL, 16, 128)
        ls[p][a, :, :, :128] = low.astype(BF16)
        high = dbuf[pl.ds(512, 256), :128].reshape(NL, 8, 128)
        tail = width - 128
        if tail > 0:
            at = lax.broadcasted_iota(jnp.int32, (512, 128), 1)
            first = jnp.where(at < tail, dbuf[pl.ds(0, 512), 128:], 0.0).reshape(NL, 16, 128)
            last = jnp.where(at[:256] < tail, dbuf[pl.ds(512, 256), 128:], 0.0)
            ends = first[:, :8] + (
                pltpu.roll(first[:, 8:].reshape(256, 128), tail, 1)
                + pltpu.roll(last, 2 * tail, 1)
            ).reshape(NL, 8, 128)
        else:
            ends = jnp.zeros((NL, 8, 128), F32)
        ls[p][a, :, :, 128:] = jnp.concatenate([high, ends], axis=1).astype(BF16)
        send_lat(a, p)

    def analyse_lat(a, p):
        count = PARTS[p][1]
        tail = WIDTH[p] - 128
        at = lanes(NL)
        wait_lat(a, p, lrs)
        dbuf[pl.ds(0, 512), :] = dot(perm[...], lr[p][a].reshape(512, 256))
        for kk in range(K):
            base, shift = divmod(SLOT * kk, 128)
            i, t = (kk, 0) if kk < 16 else (kk - 16, 1)
            main = dbuf[pl.ds(NL * i, NL), 128 * t : 128 * (t + 1)]
            main = pltpu.roll(main, shift, 1) if shift else main
            ring[kk, :, :128] = main
            if tail > 0:
                end = dbuf[pl.ds(NL * (8 + kk % 8), NL), 128:]
                turn = (shift - tail * (kk // 8)) % 128
                end = pltpu.roll(end, turn, 1) if turn else end
                ring[kk, :, 128:256] = jnp.where(at < shift, main, end) if shift else end
                ring[kk, :, 256:384] = end
            else:
                ring[kk, :, 128:256] = main
        for q in range(Q):
            start = count * q

            def pick(kk, t):
                t -= SLOT * kk // 128
                return ring[kk, :, 128 * t : 128 * (t + 1)]

            tiles = merge(NL, start, SLOT, K, pick)
            xform[pl.ds(NL * q, NL), :] = shift_left(tiles, start % 128)[:, : SLOT * K]
        strans[...] = jnp.transpose(xform[...]).astype(BF16)

    def synth_lat(p):
        count = PARTS[p][1]
        tail = WIDTH[p] - 128
        at = lanes(NL)
        xform[...] = jnp.transpose(sback[...])
        blank = jnp.zeros((NL, 128), F32)
        for q in range(Q):
            row = jnp.concatenate([xform[pl.ds(NL * q, NL), :], blank], axis=1)
            shift = count * q % 128
            ring[q] = pltpu.roll(row, shift, 1) if shift else row

        def column(kk):
            def pick(q, t):
                t -= count * q // 128
                return ring[q, :, 128 * t : 128 * (t + 1)]

            tiles = merge(NL, SLOT * kk, count, Q, pick)
            return shift_left(tiles, SLOT * kk % 128)

        for i in range(16):
            low = column(i)
            ring[Q + i % 8, :, 128 * (i // 8) : 128 * (i // 8 + 1)] = low[:, :128]
            if tail > 0:
                done = low[:, 128:256]
                if i < 8:
                    ring[Q + i, :, 256:384] = done
                else:
                    old = ring[Q + i - 8, :, 256:384]
                    ring[Q + i - 8, :, 256:384] = jnp.where(at >= tail, pltpu.roll(done, tail, 1), old)
        for i in range(8):
            high = column(16 + i)
            low = ring[Q + i, :, :128]
            xbuf[pl.ds(NL * i, NL), :] = jnp.concatenate([low, high[:, :128]], axis=1).astype(BF16)
            ends = blank
            if tail > 0:
                ends = jnp.where(
                    at >= 2 * tail, pltpu.roll(high[:, 128:256], 2 * tail, 1), ring[Q + i, :, 256:384]
                )
            low = ring[Q + i, :, 128:256]
            xbuf[pl.ds(NL * (8 + i), NL), :] = jnp.concatenate([low, ends], axis=1).astype(BF16)
        moved = dot(permt[...], xbuf[pl.ds(0, 512), :]).astype(BF16)
        ls[p][2] = moved.reshape(NL, 16, 256)
        send_lat(2, p)

    def synth_lon(p):
        width = WIDTH[p]
        tail = width - 128
        wait_lat(2, p, lrs)
        got = lr[p][2]
        xbuf[pl.ds(0, 512), :128] = got[:, :, :128].reshape(512, 128)
        second = got[:, :, 128:].astype(F32)
        xbuf[pl.ds(512, 256), :128] = second[:, :8].reshape(256, 128).astype(BF16)
        if tail > 0:
            ends = second[:, 8:].reshape(256, 128)
            one = pltpu.roll(ends, 128 - tail, 1)
            two = pltpu.roll(ends, 128 - 2 * tail, 1)
            both = jnp.concatenate([ends.reshape(NL, 8, 128), one.reshape(NL, 8, 128)], axis=1)
            xbuf[pl.ds(0, 512), 128:] = both.reshape(512, 128).astype(BF16)
            xbuf[pl.ds(512, 256), 128:] = two.astype(BF16)
        else:
            xbuf[:, 128:] = jnp.zeros((768, 128), BF16)
        at = lax.broadcasted_iota(jnp.int32, (256, 256), 1)
        tiles = [None] * TILES[p]
        for g in range(GROUPS):
            base, shift = divmod(width * g, 128)
            value = dot(bwd[pl.ds(256 * g, 256), :], xbuf[...])
            value = jnp.where(at < width, value, 0.0)
            value = pltpu.roll(value, shift, 1) if shift else value
            for t in range(2):
                if base + t < TILES[p]:
                    piece = value[:, 128 * t : 128 * (t + 1)]
                    old = tiles[base + t]
                    tiles[base + t] = piece if old is None else old + piece
        for t in range(TILES[p]):
            zs[p][2, :, :, 128 * t : 128 * (t + 1)] = tiles[t].astype(BF16).reshape(NZ, 16, 128)
        send_lon(2, p)

    def unpack(p):
        first, count = PARTS[p]
        wait_lon(2, p, zrs)
        for z in range(NZ):
            for g in range(GROUPS):
                base, shift = divmod(WIDTH[p] * g, 128)
                window = [zr[p][2, z, :, 128 * t : 128 * (t + 1)] for t in range(base, min(base + 2, TILES[p]))]
                window += [window[-1]] * (3 - len(window))
                turn = (C * z + first - shift) % RING
                wide = jnp.concatenate(window, axis=1)
                pbuf[z, 16 * g : 16 * (g + 1), :] = pltpu.roll(wide, turn, 1) if turn else wide
        at = lanes(N)
        for q in range(Q):
            start = first + count * q
            tiles = []
            for t in range(3):
                low = 128 * t - start
                z = low // C
                value = pbuf[z % NZ, :, 128 * t : 128 * (t + 1)]
                while C * (z + 1) - low < 128:
                    z += 1
                    value = jnp.where(
                        at >= C * z - low, pbuf[z % NZ, :, 128 * t : 128 * (t + 1)], value
                    )
                tiles.append(value)
            whole = shift_left(tiles, count * q)
            if p == 0:
                grad_out[q] = whole
            else:
                for t in range(3):
                    span = slice(128 * t, 128 * (t + 1))
                    inner = lax.rem(at + 128 * t, C)
                    grad_out[q, :, span] = jnp.where(inner < first, grad_out[q, :, span], whole[:, span])

    loads[0].wait()
    pack(0, 0)
    pack(0, 1)
    pl.semaphore_wait(barrier, len(greeted))
    for d in (4, 12):
        pl.semaphore_signal(far_sem, inc=1, device_id=ring_peer(d), device_id_type=MESH)
    for d in (2, 1, 3):
        pl.semaphore_signal(col_sem, inc=1, device_id=column_peer(d), device_id_type=MESH)
    send_lon(0, 0, near[::-1], False)
    pl.semaphore_wait(far_sem, 2)
    send_lon(0, 0, far)
    send_lon(0, 1)
    loads[1].wait()
    pack(1, 0)
    send_lon(1, 0)
    pack(1, 1)
    send_lon(1, 1)

    perm[...] = one_hot(512, lambda r: (r & (NL - 1)) * 16 + (r >> 5))
    permt[...] = one_hot(512, lambda r: (r & 15) * NL + (r >> 4))
    order = one_hot(LATS, lambda r: (r & (NL - 1)) * Q + (r >> 5))
    loads[2].wait()

    def reorder(m, carry):
        legp[m] = dot(order, leg[m]).astype(BF16)
        return carry

    lax.fori_loop(0, M, reorder, 0, unroll=2)
    loads[5].wait()
    gain[0] = filt[:, :SLOT]
    for r in range(2):
        first, count = PARTS[1]
        gain[1, r, :count] = filt[r, first:]
        gain[1, r, count:] = jnp.zeros((SLOT - count, DEGREES), F32)
    loads[3].wait()
    loads[4].wait()

    def spectrum(m):
        rows = pl.ds(pl.multiple_of(2 * SLOT * m, 2 * SLOT), 2 * SLOT)
        return dot(strans[rows, :], legp[m])

    def filter_cot(p):
        def analyse(m, carry):
            coef[p, m] = spectrum(m)
            return carry

        lax.fori_loop(0, M, analyse, 0, unroll=4)

        def synth(m, carry):
            re, im = coef[p, m, :SLOT], coef[p, m, SLOT:]
            back = jnp.concatenate(
                [gain[p, 0] * re + gain[p, 1] * im, gain[p, 0] * im - gain[p, 1] * re], axis=0
            ).astype(BF16)
            rows = pl.ds(pl.multiple_of(2 * SLOT * m, 2 * SLOT), 2 * SLOT)
            sback[rows, :] = lax.dot_general(
                back, legp[m], (((1,), (1,)), ((), ())), preferred_element_type=F32
            )
            return carry

        lax.fori_loop(0, M, synth, 0, unroll=4)

    def correlate(p):
        def one(m, carry):
            got = spectrum(m)
            in_re, in_im = got[:SLOT], got[SLOT:]
            cot_re, cot_im = coef[p, m, :SLOT], coef[p, m, SLOT:]
            acc[pl.ds(2 * SLOT * p, SLOT), :] += in_re * cot_re + in_im * cot_im
            acc[pl.ds(2 * SLOT * p + SLOT, SLOT), :] += in_re * cot_im - in_im * cot_re
            return carry

        lax.fori_loop(0, M, one, 0, unroll=4)

    acc[...] = jnp.zeros_like(acc)
    pl.semaphore_wait(col_sem, 3)
    analyse_lon(0, 0)
    analyse_lat(0, 0)
    analyse_lon(0, 1)
    filter_cot(0)
    synth_lat(0)
    analyse_lat(0, 1)
    filter_cot(1)
    synth_lat(1)
    synth_lon(0)
    analyse_lon(1, 0)
    synth_lon(1)
    analyse_lon(1, 1)
    analyse_lat(1, 0)
    correlate(0)
    analyse_lat(1, 1)
    correlate(1)
    gs[...] = jnp.transpose(acc[...])

    def send_sum(s, carry):
        to = lat ^ (NL - 1 - s)
        start = pl.multiple_of(Q * to - 4 * lax.rem(to, 2), 8)
        pltpu.make_async_remote_copy(
            src_ref=gs.at[pl.ds(start, 16)],
            dst_ref=gr.at[lat],
            send_sem=gss,
            recv_sem=grs,
            device_id=(to, lon),
            device_id_type=MESH,
        ).start()
        return carry

    lax.fori_loop(0, NL - 1, send_sum, 0)
    start = pl.multiple_of(Q * lat - 4 * lax.rem(lat, 2), 8)
    own = pltpu.make_async_copy(gs.at[pl.ds(start, 16)], gr.at[lat], own_sem.at[0])
    own.start()
    own.wait()
    some = gr.at[pl.ds(0, NL - 1)]
    unpack(0)
    pltpu.make_async_copy(some, some, grs).wait()
    total = jnp.sum(gr[...], axis=0)
    total = jnp.where(lax.rem(lat, 2) == 1, total[4:16], total[:12])
    for r in range(2):
        for p in range(2):
            first, count = PARTS[p]
            low = 2 * SLOT * p + SLOT * r
            filt_out[:, r, first : first + count] = total[:, low : low + count]
    for phase in range(3):
        for p in range(2):
            if (phase, p) != (2, 1):
                wait_lon(phase, p, zss)
            wait_lat(phase, p, lss)
    pltpu.make_async_copy(some, some, gss).wait()
    unpack(1)
    wait_lon(2, 1, zss)


def hand_over(grad_in, filt_in, grad_out, filt_out, sem):
    copies = [
        pltpu.make_async_copy(grad_in, grad_out, sem.at[0]),
        pltpu.make_async_copy(filt_in, filt_out, sem.at[1]),
    ]
    for copy in copies:
        copy.start()
    for copy in copies:
        copy.wait()


def local(grid_in, grid_cot, legendre, filters):
    fwd, bwd = fourier_tables()
    vmem = pltpu.VMEM
    any_space = pl.BlockSpec(memory_space=pl.ANY)
    outs = pl.pallas_call(
        kernel,
        out_shape=(vmem((Q, N, CHANNELS), BF16), vmem((Q, 2, C), F32)),
        in_specs=[any_space] * 6,
        out_specs=(pl.BlockSpec(memory_space=vmem), pl.BlockSpec(memory_space=vmem)),
        scratch_shapes=[
            vmem((2, Q, N, CHANNELS), BF16),
            vmem((M, LATS, DEGREES), BF16),
            vmem((M, LATS, DEGREES), BF16),
            vmem((2, C, DEGREES), F32),
            vmem((2 * DEGREES, LONS), BF16),
            vmem((LONS, 2 * DEGREES), BF16),
            vmem((512, 512), BF16),
            vmem((512, 512), BF16),
            vmem((K, NL, 512), F32),
            vmem((NZ, N, RING), BF16),
            vmem((2, 2, SLOT, DEGREES), F32),
            vmem((768, 256), BF16),
            vmem((768, 256), F32),
            vmem((LATS, SLOT * K), F32),
            vmem((SLOT * K, LATS), BF16),
            vmem((SLOT * K, LATS), F32),
            vmem((2, M, 2 * SLOT, DEGREES), F32),
            vmem((128, DEGREES), F32),
            vmem((3, NZ, 16, 128 * TILES[0]), BF16),
            vmem((3, NZ, 16, 128 * TILES[1]), BF16),
            vmem((3, NZ, 16, 128 * TILES[0]), BF16),
            vmem((3, NZ, 16, 128 * TILES[1]), BF16),
            vmem((3, NL, 16, 256), BF16),
            vmem((3, NL, 16, 256), BF16),
            vmem((3, NL, 16, 256), BF16),
            vmem((3, NL, 16, 256), BF16),
            vmem((DEGREES, 128), F32),
            vmem((NL, 16, 128), F32),
            pltpu.SemaphoreType.DMA((6,)),
            pltpu.SemaphoreType.DMA((1,)),
            pltpu.SemaphoreType.DMA((3, 2)),
            pltpu.SemaphoreType.DMA((3, 2)),
            pltpu.SemaphoreType.DMA((3, 2)),
            pltpu.SemaphoreType.DMA((3, 2)),
            pltpu.SemaphoreType.DMA,
            pltpu.SemaphoreType.DMA,
            pltpu.SemaphoreType.REGULAR,
            pltpu.SemaphoreType.REGULAR,
        ],
        compiler_params=pltpu.CompilerParams(
            collective_id=0, has_side_effects=True, vmem_limit_bytes=56 * 1024 * 1024
        ),
    )(
        grid_in, grid_cot, legendre, jnp.transpose(filters, (1, 2, 0)), jnp.asarray(fwd), jnp.asarray(bwd)
    )
    held = [pltpu.with_memory_space_constraint(out, pltpu.VMEM) for out in outs]
    return pl.pallas_call(
        hand_over,
        out_shape=(
            jax.ShapeDtypeStruct((Q, N, CHANNELS), BF16),
            jax.ShapeDtypeStruct((Q, 2, C), F32),
        ),
        in_specs=[pl.BlockSpec(memory_space=vmem)] * 2,
        out_specs=(any_space, any_space),
        scratch_shapes=[pltpu.SemaphoreType.DMA((2,))],
    )(*held)


def solution(mesh):
    return jax.shard_map(
        local,
        mesh=mesh,
        in_specs=(
            P("lat", "lon", None),
            P("lat", "lon", None),
            P("lat", None, None),
            P(None, None, "lon"),
        ),
        out_specs=(P("lat", "lon", None), P("lat", None, "lon")),
        check_vma=False,
    )
```

```python
import math

import jax
import jax.numpy as jnp
import ml_dtypes
import numpy as np
from jax import lax
from jax.experimental import pallas as pl
from jax.experimental.pallas import tpu as pltpu
from jax.sharding import PartitionSpec as P

MESH = pl.DeviceIdType.MESH
BF16 = jnp.bfloat16
F32 = jnp.float32

NZ, NL = 16, 32
LATS, LONS, DEGREES, CHANNELS = 384, 768, 384, 384
Q, N, C = LATS // NL, LONS // NZ, CHANNELS // NZ
M = DEGREES // NL
K = 2 * M
RING = 384
GROUPS = N // 16
SLOT = 16

PARTS = ((0, 14), (14, 10))
WIDTH = tuple(Q * count for _, count in PARTS)
TILES = tuple(-(-GROUPS * w // 128) for w in WIDTH)


def fourier_tables():
    points = np.arange(LONS, dtype=np.int64)[:, None]
    order = np.arange(DEGREES, dtype=np.int64)[None, :]
    phases = (points * order) % LONS
    angles = phases.astype(np.float32) * np.float32(2.0 * math.pi / LONS)
    pair = np.stack([np.cos(angles), -np.sin(angles)], axis=2) * np.float32(LONS ** (-0.5))
    table = pair.reshape(LONS, 2 * DEGREES).astype(ml_dtypes.bfloat16)
    n_of = np.arange(LONS).reshape(NZ, GROUPS, 16).transpose(1, 0, 2).reshape(-1)
    k = np.arange(2 * DEGREES).reshape(NL, 2 * M)
    k_of = np.concatenate([k[:, :16].reshape(-1), k[:, 16:].reshape(-1)])
    back = table[n_of][:, k_of]
    return np.ascontiguousarray(back.T), np.ascontiguousarray(back)


def lanes(rows):
    return lax.broadcasted_iota(jnp.int32, (rows, 128), 1)


def merge(rows, start, step, count, pick):
    at = lanes(rows)
    tiles = []
    for t in range(start // 128, (start + step * count - 1) // 128 + 1):
        value = None
        for i in range(count):
            low, high = start + step * i - 128 * t, start + step * (i + 1) - 128 * t
            if high <= 0 or low >= 128:
                continue
            block = pick(i, t)
            value = block if value is None else jnp.where(at >= low, block, value)
        tiles.append(value)
    return tiles


def shift_left(tiles, shift):
    wide = jnp.concatenate(tiles, axis=1) if len(tiles) > 1 else tiles[0]
    size = 128 * len(tiles)
    return pltpu.roll(wide, (size - shift) % size, 1) if shift % size else wide


def grid_row(pbuf, p, q):
    first, count = PARTS[p]
    at = lanes(N)
    start = first + count * q
    tiles = []
    for t in range(3):
        low = 128 * t - start
        z = low // C
        value = pbuf[z % NZ, :, 128 * t : 128 * (t + 1)]
        while C * (z + 1) - low < 128:
            z += 1
            value = jnp.where(at >= C * z - low, pbuf[z % NZ, :, 128 * t : 128 * (t + 1)], value)
        tiles.append(value)
    return shift_left(tiles, count * q)


def one_hot(size, column_of):
    row = lax.broadcasted_iota(jnp.int32, (size, size), 0)
    column = lax.broadcasted_iota(jnp.int32, (size, size), 1)
    return jnp.where(column == column_of(row), 1.0, 0.0).astype(BF16)


def dot(a, b):
    return jnp.dot(a, b, preferred_element_type=F32)


def kernel(
    in_hbm, cot_hbm, leg_hbm, filt_hbm, fwd_hbm, bwd_hbm,
    grad_out, filt_out, pbuf,
    grid, leg, legp, filt, fwd, bwd, perm, permt, ring, gain, xbuf, dbuf, xform, strans, sback, coef, acc,
    zs_a, zs_b, zr_a, zr_b, ls_a, ls_b, lr_a, lr_b, gs, gr,
    load_sem, own_sem, zss, zrs, lss, lrs, gss, grs, far_sem, col_sem,
):
    lat, lon = lax.axis_index("lat"), lax.axis_index("lon")
    zs, zr, ls, lr = (zs_a, zs_b), (zr_a, zr_b), (ls_a, ls_b), (lr_a, lr_b)

    def ring_peer(d):
        return (lat, lax.rem(lon + d, NZ))

    def row_peer(d):
        return ((lat & 6) | ((lat ^ d) & 25), lon)

    def column_peer(d):
        return ((lat & 25) | ((lat + 2 * d) & 6), lon)

    barrier = pltpu.get_barrier_semaphore()
    near = (4, 12, 3, 13, 2, 14, 1, 15)
    far = (8, 7, 9, 6, 10, 5, 11)
    greeted = [ring_peer(d) for d in near]
    greeted += [row_peer(d) for d in (25, 24, 17, 16, 9, 8, 1)]
    greeted += [column_peer(d) for d in (2, 1, 3)]
    for peer in greeted:
        pl.semaphore_signal(barrier, inc=1, device_id=peer, device_id_type=MESH)
    loads = [
        pltpu.make_async_copy(cot_hbm, grid.at[0], load_sem.at[0]),
        pltpu.make_async_copy(in_hbm, grid.at[1], load_sem.at[1]),
        pltpu.make_async_copy(leg_hbm, leg, load_sem.at[2]),
        pltpu.make_async_copy(fwd_hbm, fwd, load_sem.at[3]),
        pltpu.make_async_copy(bwd_hbm, bwd, load_sem.at[4]),
        pltpu.make_async_copy(filt_hbm, filt, load_sem.at[5]),
    ]
    for load in loads:
        load.start()
    def send_lon(phase, p, distances=far + near, own=True):
        for d in distances:
            to = lax.rem(lon + d, NZ)
            pltpu.make_async_remote_copy(
                src_ref=zs[p].at[phase, to],
                dst_ref=zr[p].at[phase, lon],
                send_sem=zss.at[phase, p],
                recv_sem=zrs.at[phase, p],
                device_id=(lat, to),
                device_id_type=MESH,
            ).start()
        if own:
            zr[p][phase, lon] = zs[p][phase, lon]

    def wait_lon(phase, p, sem):
        some = zr[p].at[phase, pl.ds(0, NZ - 1)]
        pltpu.make_async_copy(some, some, sem.at[phase, p]).wait()

    def send_lat(phase, p):
        def step(s, carry):
            to = lat ^ (NL - 1 - s)
            pltpu.make_async_remote_copy(
                src_ref=ls[p].at[phase, to],
                dst_ref=lr[p].at[phase, lat],
                send_sem=lss.at[phase, p],
                recv_sem=lrs.at[phase, p],
                device_id=(to, lon),
                device_id_type=MESH,
            ).start()
            return carry

        lax.fori_loop(0, NL - 1, step, 0)
        lr[p][phase, lat] = ls[p][phase, lat]

    def wait_lat(phase, p, sem):
        some = lr[p].at[phase, pl.ds(0, NL - 1)]
        pltpu.make_async_copy(some, some, sem.at[phase, p]).wait()

    def pack(a, p):
        first, count = PARTS[p]
        at = lanes(16)
        for q in range(Q):
            wide = grid[a, q]
            pbuf[q] = pltpu.roll(wide, count * q, 1) if q else wide
        for z in range(NZ):
            start = C * z + first
            moved = jnp.concatenate(
                merge(N, start, count, Q, lambda q, t: pbuf[q, :, 128 * (t % 3) : 128 * (t % 3) + 128]),
                axis=1,
            )
            size = moved.shape[1]
            if size == 128:
                moved = jnp.concatenate([moved, moved], axis=1)
                size = 256
            tiles = [None] * (TILES[p] + 1)
            for g in range(GROUPS):
                base, shift = divmod(WIDTH[p] * g, 128)
                turn = (shift - start % 128) % size
                rows = moved[16 * g : 16 * (g + 1)]
                rows = pltpu.roll(rows, turn, 1) if turn else rows
                old = tiles[base]
                tiles[base] = rows[:, :128] if old is None else jnp.where(at >= shift, rows[:, :128], old)
                tiles[base + 1] = rows[:, 128:256]
            zs[p][a, z] = jnp.concatenate(tiles[: TILES[p]], axis=1)

    def analyse_lon(a, p):
        width = WIDTH[p]
        wait_lon(a, p, zrs)
        for g in range(GROUPS):
            base, shift = divmod(width * g, 128)
            window = zr[p][a, :, :, 128 * base : 128 * base + 256].reshape(256, 256)
            if shift:
                window = pltpu.roll(window.astype(F32), 256 - shift, 1).astype(BF16)
            xbuf[pl.ds(256 * g, 256), :] = window
        for r in range(3):
            dbuf[pl.ds(256 * r, 256), :] = dot(fwd[pl.ds(256 * r, 256), :], xbuf[...])
        low = dbuf[pl.ds(0, 512), :128].reshape(NL, 16, 128)
        ls[p][a, :, :, :128] = low.astype(BF16)
        high = dbuf[pl.ds(512, 256), :128].reshape(NL, 8, 128)
        tail = width - 128
        if tail > 0:
            at = lax.broadcasted_iota(jnp.int32, (512, 128), 1)
            first = jnp.where(at < tail, dbuf[pl.ds(0, 512), 128:], 0.0).reshape(NL, 16, 128)
            last = jnp.where(at[:256] < tail, dbuf[pl.ds(512, 256), 128:], 0.0)
            ends = first[:, :8] + (
                pltpu.roll(first[:, 8:].reshape(256, 128), tail, 1)
                + pltpu.roll(last, 2 * tail, 1)
            ).reshape(NL, 8, 128)
        else:
            ends = jnp.zeros((NL, 8, 128), F32)
        ls[p][a, :, :, 128:] = jnp.concatenate([high, ends], axis=1).astype(BF16)
        send_lat(a, p)

    def analyse_lat(a, p):
        count = PARTS[p][1]
        tail = WIDTH[p] - 128
        at = lanes(NL)
        wait_lat(a, p, lrs)
        dbuf[pl.ds(0, 512), :] = dot(perm[...], lr[p][a].reshape(512, 256))
        for kk in range(K):
            base, shift = divmod(SLOT * kk, 128)
            i, t = (kk, 0) if kk < 16 else (kk - 16, 1)
            main = dbuf[pl.ds(NL * i, NL), 128 * t : 128 * (t + 1)]
            main = pltpu.roll(main, shift, 1) if shift else main
            ring[kk, :, :128] = main
            if tail > 0:
                end = dbuf[pl.ds(NL * (8 + kk % 8), NL), 128:]
                turn = (shift - tail * (kk // 8)) % 128
                end = pltpu.roll(end, turn, 1) if turn else end
                ring[kk, :, 128:256] = jnp.where(at < shift, main, end) if shift else end
                ring[kk, :, 256:384] = end
            else:
                ring[kk, :, 128:256] = main
        for q in range(Q):
            start = count * q

            def pick(kk, t):
                t -= SLOT * kk // 128
                return ring[kk, :, 128 * t : 128 * (t + 1)]

            tiles = merge(NL, start, SLOT, K, pick)
            xform[pl.ds(NL * q, NL), :] = shift_left(tiles, start % 128)[:, : SLOT * K]
        strans[...] = jnp.transpose(xform[...]).astype(BF16)

    def synth_lat(p):
        count = PARTS[p][1]
        tail = WIDTH[p] - 128
        at = lanes(NL)
        xform[...] = jnp.transpose(sback[...])
        blank = jnp.zeros((NL, 128), F32)
        for q in range(Q):
            row = jnp.concatenate([xform[pl.ds(NL * q, NL), :], blank], axis=1)
            shift = count * q % 128
            ring[q] = pltpu.roll(row, shift, 1) if shift else row

        def column(kk):
            def pick(q, t):
                t -= count * q // 128
                return ring[q, :, 128 * t : 128 * (t + 1)]

            tiles = merge(NL, SLOT * kk, count, Q, pick)
            return shift_left(tiles, SLOT * kk % 128)

        for i in range(16):
            low = column(i)
            ring[Q + i % 8, :, 128 * (i // 8) : 128 * (i // 8 + 1)] = low[:, :128]
            if tail > 0:
                done = low[:, 128:256]
                if i < 8:
                    ring[Q + i, :, 256:384] = done
                else:
                    old = ring[Q + i - 8, :, 256:384]
                    ring[Q + i - 8, :, 256:384] = jnp.where(at >= tail, pltpu.roll(done, tail, 1), old)
        for i in range(8):
            high = column(16 + i)
            low = ring[Q + i, :, :128]
            xbuf[pl.ds(NL * i, NL), :] = jnp.concatenate([low, high[:, :128]], axis=1).astype(BF16)
            ends = blank
            if tail > 0:
                ends = jnp.where(
                    at >= 2 * tail, pltpu.roll(high[:, 128:256], 2 * tail, 1), ring[Q + i, :, 256:384]
                )
            low = ring[Q + i, :, 128:256]
            xbuf[pl.ds(NL * (8 + i), NL), :] = jnp.concatenate([low, ends], axis=1).astype(BF16)
        moved = dot(permt[...], xbuf[pl.ds(0, 512), :]).astype(BF16)
        ls[p][2] = moved.reshape(NL, 16, 256)
        send_lat(2, p)

    def synth_lon(p):
        width = WIDTH[p]
        tail = width - 128
        wait_lat(2, p, lrs)
        got = lr[p][2]
        xbuf[pl.ds(0, 512), :128] = got[:, :, :128].reshape(512, 128)
        second = got[:, :, 128:].astype(F32)
        xbuf[pl.ds(512, 256), :128] = second[:, :8].reshape(256, 128).astype(BF16)
        if tail > 0:
            ends = second[:, 8:].reshape(256, 128)
            one = pltpu.roll(ends, 128 - tail, 1)
            two = pltpu.roll(ends, 128 - 2 * tail, 1)
            both = jnp.concatenate([ends.reshape(NL, 8, 128), one.reshape(NL, 8, 128)], axis=1)
            xbuf[pl.ds(0, 512), 128:] = both.reshape(512, 128).astype(BF16)
            xbuf[pl.ds(512, 256), 128:] = two.astype(BF16)
        else:
            xbuf[:, 128:] = jnp.zeros((768, 128), BF16)
        at = lax.broadcasted_iota(jnp.int32, (256, 256), 1)
        tiles = [None] * TILES[p]
        for g in range(GROUPS):
            base, shift = divmod(width * g, 128)
            value = dot(bwd[pl.ds(256 * g, 256), :], xbuf[...])
            value = jnp.where(at < width, value, 0.0)
            value = pltpu.roll(value, shift, 1) if shift else value
            for t in range(2):
                if base + t < TILES[p]:
                    piece = value[:, 128 * t : 128 * (t + 1)]
                    old = tiles[base + t]
                    tiles[base + t] = piece if old is None else old + piece
        for t in range(TILES[p]):
            zs[p][2, :, :, 128 * t : 128 * (t + 1)] = tiles[t].astype(BF16).reshape(NZ, 16, 128)
        send_lon(2, p)

    def unpack(p):
        first, count = PARTS[p]
        wait_lon(2, p, zrs)
        for z in range(NZ):
            for g in range(GROUPS):
                base, shift = divmod(WIDTH[p] * g, 128)
                window = [zr[p][2, z, :, 128 * t : 128 * (t + 1)] for t in range(base, min(base + 2, TILES[p]))]
                window += [window[-1]] * (3 - len(window))
                turn = (C * z + first - shift) % RING
                wide = jnp.concatenate(window, axis=1)
                pbuf[z, 16 * g : 16 * (g + 1), :] = pltpu.roll(wide, turn, 1) if turn else wide
        if p == 0:
            for q in range(Q):
                grad_out[q] = grid_row(pbuf, p, q)

    loads[0].wait()
    pack(0, 0)
    pack(0, 1)
    pl.semaphore_wait(barrier, len(greeted))
    for d in (4, 12):
        pl.semaphore_signal(far_sem, inc=1, device_id=ring_peer(d), device_id_type=MESH)
    for d in (2, 1, 3):
        pl.semaphore_signal(col_sem, inc=1, device_id=column_peer(d), device_id_type=MESH)
    send_lon(0, 0, near[::-1], False)
    pl.semaphore_wait(far_sem, 2)
    send_lon(0, 0, far)
    send_lon(0, 1)
    loads[1].wait()
    pack(1, 0)
    send_lon(1, 0)
    pack(1, 1)
    send_lon(1, 1)

    perm[...] = one_hot(512, lambda r: (r & (NL - 1)) * 16 + (r >> 5))
    permt[...] = one_hot(512, lambda r: (r & 15) * NL + (r >> 4))
    order = one_hot(LATS, lambda r: (r & (NL - 1)) * Q + (r >> 5))
    loads[2].wait()

    def reorder(m, carry):
        legp[m] = dot(order, leg[m]).astype(BF16)
        return carry

    lax.fori_loop(0, M, reorder, 0, unroll=2)
    loads[5].wait()
    gain[0] = filt[:, :SLOT]
    for r in range(2):
        first, count = PARTS[1]
        gain[1, r, :count] = filt[r, first:]
        gain[1, r, count:] = jnp.zeros((SLOT - count, DEGREES), F32)
    loads[3].wait()
    loads[4].wait()

    def spectrum(m):
        rows = pl.ds(pl.multiple_of(2 * SLOT * m, 2 * SLOT), 2 * SLOT)
        return dot(strans[rows, :], legp[m])

    def filter_cot(p):
        def analyse(m, carry):
            coef[p, m] = spectrum(m)
            return carry

        lax.fori_loop(0, M, analyse, 0, unroll=4)

        def synth(m, carry):
            re, im = coef[p, m, :SLOT], coef[p, m, SLOT:]
            back = jnp.concatenate(
                [gain[p, 0] * re + gain[p, 1] * im, gain[p, 0] * im - gain[p, 1] * re], axis=0
            ).astype(BF16)
            rows = pl.ds(pl.multiple_of(2 * SLOT * m, 2 * SLOT), 2 * SLOT)
            sback[rows, :] = lax.dot_general(
                back, legp[m], (((1,), (1,)), ((), ())), preferred_element_type=F32
            )
            return carry

        lax.fori_loop(0, M, synth, 0, unroll=4)

    def correlate(p):
        def one(m, carry):
            got = spectrum(m)
            in_re, in_im = got[:SLOT], got[SLOT:]
            cot_re, cot_im = coef[p, m, :SLOT], coef[p, m, SLOT:]
            acc[pl.ds(2 * SLOT * p, SLOT), :] += in_re * cot_re + in_im * cot_im
            acc[pl.ds(2 * SLOT * p + SLOT, SLOT), :] += in_re * cot_im - in_im * cot_re
            return carry

        lax.fori_loop(0, M, one, 0, unroll=4)

    acc[...] = jnp.zeros_like(acc)
    pl.semaphore_wait(col_sem, 3)
    analyse_lon(0, 0)
    analyse_lat(0, 0)
    analyse_lon(0, 1)
    filter_cot(0)
    synth_lat(0)
    analyse_lat(0, 1)
    filter_cot(1)
    synth_lat(1)
    synth_lon(0)
    analyse_lon(1, 0)
    synth_lon(1)
    analyse_lon(1, 1)
    analyse_lat(1, 0)
    correlate(0)
    analyse_lat(1, 1)
    correlate(1)
    gs[...] = jnp.transpose(acc[...])

    def send_sum(s, carry):
        to = lat ^ (NL - 1 - s)
        start = pl.multiple_of(Q * to - 4 * lax.rem(to, 2), 8)
        pltpu.make_async_remote_copy(
            src_ref=gs.at[pl.ds(start, 16)],
            dst_ref=gr.at[lat],
            send_sem=gss,
            recv_sem=grs,
            device_id=(to, lon),
            device_id_type=MESH,
        ).start()
        return carry

    lax.fori_loop(0, NL - 1, send_sum, 0)
    start = pl.multiple_of(Q * lat - 4 * lax.rem(lat, 2), 8)
    own = pltpu.make_async_copy(gs.at[pl.ds(start, 16)], gr.at[lat], own_sem.at[0])
    own.start()
    own.wait()
    some = gr.at[pl.ds(0, NL - 1)]
    unpack(0)
    pltpu.make_async_copy(some, some, grs).wait()
    total = jnp.sum(gr[...], axis=0)
    total = jnp.where(lax.rem(lat, 2) == 1, total[4:16], total[:12])
    for r in range(2):
        for p in range(2):
            first, count = PARTS[p]
            low = 2 * SLOT * p + SLOT * r
            filt_out[:, r, first : first + count] = total[:, low : low + count]
    for phase in range(3):
        for p in range(2):
            if (phase, p) != (2, 1):
                wait_lon(phase, p, zss)
            wait_lat(phase, p, lss)
    pltpu.make_async_copy(some, some, gss).wait()
    unpack(1)
    wait_lon(2, 1, zss)


def hand_over(grad_in, filt_in, pbuf, grad_out, filt_out, row, sem):
    first = PARTS[1][0]
    at = lanes(N)
    copies = [pltpu.make_async_copy(filt_in, filt_out, sem.at[Q])]
    copies[0].start()
    for q in range(Q):
        whole = grid_row(pbuf, 1, q)
        for t in range(3):
            span = slice(128 * t, 128 * (t + 1))
            inner = lax.rem(at + 128 * t, C)
            row[q, :, span] = jnp.where(inner < first, grad_in[q, :, span], whole[:, span])
        copy = pltpu.make_async_copy(row.at[q], grad_out.at[q], sem.at[q])
        copy.start()
        copies.append(copy)
    for copy in copies:
        copy.wait()


def local(grid_in, grid_cot, legendre, filters):
    fwd, bwd = fourier_tables()
    vmem = pltpu.VMEM
    any_space = pl.BlockSpec(memory_space=pl.ANY)
    outs = pl.pallas_call(
        kernel,
        out_shape=(vmem((Q, N, CHANNELS), BF16), vmem((Q, 2, C), F32), vmem((NZ, N, RING), BF16)),
        in_specs=[any_space] * 6,
        out_specs=(pl.BlockSpec(memory_space=vmem),) * 3,
        scratch_shapes=[
            vmem((2, Q, N, CHANNELS), BF16),
            vmem((M, LATS, DEGREES), BF16),
            vmem((M, LATS, DEGREES), BF16),
            vmem((2, C, DEGREES), F32),
            vmem((2 * DEGREES, LONS), BF16),
            vmem((LONS, 2 * DEGREES), BF16),
            vmem((512, 512), BF16),
            vmem((512, 512), BF16),
            vmem((K, NL, 512), F32),
            vmem((2, 2, SLOT, DEGREES), F32),
            vmem((768, 256), BF16),
            vmem((768, 256), F32),
            vmem((LATS, SLOT * K), F32),
            vmem((SLOT * K, LATS), BF16),
            vmem((SLOT * K, LATS), F32),
            vmem((2, M, 2 * SLOT, DEGREES), F32),
            vmem((128, DEGREES), F32),
            vmem((3, NZ, 16, 128 * TILES[0]), BF16),
            vmem((3, NZ, 16, 128 * TILES[1]), BF16),
            vmem((3, NZ, 16, 128 * TILES[0]), BF16),
            vmem((3, NZ, 16, 128 * TILES[1]), BF16),
            vmem((3, NL, 16, 256), BF16),
            vmem((3, NL, 16, 256), BF16),
            vmem((3, NL, 16, 256), BF16),
            vmem((3, NL, 16, 256), BF16),
            vmem((DEGREES, 128), F32),
            vmem((NL, 16, 128), F32),
            pltpu.SemaphoreType.DMA((6,)),
            pltpu.SemaphoreType.DMA((1,)),
            pltpu.SemaphoreType.DMA((3, 2)),
            pltpu.SemaphoreType.DMA((3, 2)),
            pltpu.SemaphoreType.DMA((3, 2)),
            pltpu.SemaphoreType.DMA((3, 2)),
            pltpu.SemaphoreType.DMA,
            pltpu.SemaphoreType.DMA,
            pltpu.SemaphoreType.REGULAR,
            pltpu.SemaphoreType.REGULAR,
        ],
        compiler_params=pltpu.CompilerParams(
            collective_id=0, has_side_effects=True, vmem_limit_bytes=56 * 1024 * 1024
        ),
    )(
        grid_in, grid_cot, legendre, jnp.transpose(filters, (1, 2, 0)), jnp.asarray(fwd), jnp.asarray(bwd)
    )
    held = [pltpu.with_memory_space_constraint(out, pltpu.VMEM) for out in outs]
    return pl.pallas_call(
        hand_over,
        out_shape=(
            jax.ShapeDtypeStruct((Q, N, CHANNELS), BF16),
            jax.ShapeDtypeStruct((Q, 2, C), F32),
        ),
        in_specs=[pl.BlockSpec(memory_space=vmem)] * 3,
        out_specs=(any_space, any_space),
        scratch_shapes=[vmem((Q, N, CHANNELS), BF16), pltpu.SemaphoreType.DMA((Q + 1,))],
    )(*held)


def solution(mesh):
    return jax.shard_map(
        local,
        mesh=mesh,
        in_specs=(
            P("lat", "lon", None),
            P("lat", "lon", None),
            P("lat", None, None),
            P(None, None, "lon"),
        ),
        out_specs=(P("lat", "lon", None), P("lat", None, "lon")),
        check_vma=False,
    )
```
